32 devices in a mesh: seq: 4 (over z), ctx: 8 (over y, x, core).
Axes of the slice: x: 2, y: 2, z: 4, core: 2. Of those that a mesh axis runs over, the one named last changes fastest.
Arguments:
- tokens_in: bfloat16 [4, 2048, 1600], P('seq', 'ctx'), may hold values from -6 to 6
- block_index: int32 [16], replicated, may hold values from 0 to 15, each once
- norm_gains: float32 [2, 1600], replicated, may hold values from 0.1 to 1.9
- norm_shifts: float32 [2, 1600], replicated, may hold values from -1.75 to 1.75
- w_qkv: bfloat16 [4800, 1600], P('seq'), may hold values from -0.15625 to 0.15625
- bias_model: float32 [4, 1600], replicated, may hold values from -1.75 to 1.75
- w_out: bfloat16 [1600, 1600], P('seq'), may hold values from -0.625 to 0.625
- w_up: bfloat16 [6400, 1600], P('seq'), may hold values from -0.15625 to 0.15625
- bias_up: float32 [6400], replicated, may hold values from -1.75 to 1.75
- w_down: bfloat16 [1600, 6400], P('seq'), may hold values from -0.078125 to 0.078125
- cotangent: bfloat16 [4, 2048, 1600], P('seq', 'ctx'), may hold values from -6 to 6
Outputs:
- tokens_out: bfloat16 [4, 2048, 1600], P('seq', 'ctx')
- grad_tokens: float32 [4, 2048, 1600], P('seq', 'ctx')
- grad_norm_gains: float32 [2, 1600], replicated
- grad_norm_shifts: float32 [2, 1600], replicated
- grad_w_qkv: float32 [4800, 1600], P('seq')
- grad_bias_model: float32 [4, 1600], replicated
- grad_w_out: float32 [1600, 1600], P('seq')
- grad_w_up: float32 [6400, 1600], P('seq')
- grad_bias_up: float32 [6400], replicated
- grad_w_down: float32 [1600, 6400], P('seq')
The draws below stay inside these ranges and needn't reach their ends.
Inputs may be any that keep to these rules, and one draw needn't show every extreme that they name: Stored half-block b, rows b * 128 to (b + 1) * 128 - 1 of a sequence, holds positions block_index[b] * 128 onward; each number appears once.
All inputs are finite; a program needn't handle non-finite values.
Results may differ from the reference program's by a relative error of at most 0.017.
Values may be sent and summed in bfloat16 or wider, within the bound.
No kernel may reach another device: no remote copies, remote signals or barrier semaphores. Data moves between devices by JAX's collectives and lax.ppermute only.
A program may use at most 320 MiB of HBM per device.

```python
import math
import jax
import jax.numpy as jnp
from jax import lax

D = 1600
HEADS = 25
HEAD_DIM = 64
FF = 6400
HALF = 128
LEN = 2048
SEQS = 4
BLOCKS = 16


def levels(stream_key, extent, split, low, largest):
    gain, own = 1.0, jax.random.fold_in(stream_key, 6)
    for position, parts in split:
        heights = jnp.exp(jax.random.uniform(jax.random.fold_in(own, position), (parts,), jnp.float32, low / len(split), largest / len(split)))
        gain = gain * jnp.repeat(heights, extent[position] // parts).reshape([-1 if axis == position else 1 for axis in range(len(extent))])
    return gain


def centred(stream_key, dims, width, bound, cuts=(), held_as=jnp.bfloat16):
    loudness = levels(stream_key, dims, cuts, -0.22, 0.18) if cuts else 1.0
    values = jax.random.normal(stream_key, dims, jnp.float32) * width * loudness
    return jnp.minimum(jnp.maximum(values, -bound), bound).astype(held_as)


def setup_inputs(seed: int = 0) -> dict:
    key_list = jax.random.split(jax.random.key(seed), 12)
    tokens_in = centred(key_list[0], (SEQS, LEN, D), 1.0, 6.0, ((0, 4), (1, 8)))
    block_index = jax.random.permutation(key_list[1], BLOCKS).astype(jnp.int32)
    norm_gains = jnp.clip(1.0 + 0.18 * jax.random.normal(key_list[2], (2, D), jnp.float32), 0.1, 1.9)
    norm_shifts = centred(key_list[3], (2, D), 0.3, 1.75, (), jnp.float32)
    w_qkv = centred(key_list[4], (3 * D, D), D ** -0.5, 0.15625, ((0, 4),))
    bias_model = centred(key_list[5], (4, D), 0.3, 1.75, (), jnp.float32)
    w_out = centred(key_list[6], (D, D), (D // 16) ** -0.5, 0.625, ((0, 4),))
    w_up = centred(key_list[7], (FF, D), D ** -0.5, 0.15625, ((0, 4),))
    bias_up = centred(key_list[8], (FF,), 0.3, 1.75, (), jnp.float32)
    w_down = centred(key_list[9], (D, FF), FF ** -0.5, 0.078125, ((0, 4),))
    cotangent = centred(key_list[10], (SEQS, LEN, D), 1.0, 6.0, ((0, 4), (1, 8)))
    return {"tokens_in": tokens_in, "block_index": block_index, "norm_gains": norm_gains, "norm_shifts": norm_shifts, "w_qkv": w_qkv, "bias_model": bias_model, "w_out": w_out, "w_up": w_up, "bias_up": bias_up, "w_down": w_down, "cotangent": cotangent}


@jax.custom_vjp
def low(v):
    return lax.optimization_barrier(v.astype(jnp.bfloat16)).astype(jnp.float32)

@jax.custom_vjp
def low_back(v):
    return v

def low_keep(v):
    return (low(v), None)

def low_pass(kept, grad):
    return (grad,)

def back_keep(v):
    return (v, None)

def back_low(kept, grad):
    return (low(grad),)
low.defvjp(low_keep, low_pass)
low_back.defvjp(back_keep, back_low)

def matmul(left, right):
    return jnp.dot(left, right, precision=lax.Precision.HIGHEST, preferred_element_type=jnp.float32)

def layer_norm(values, gain_row, offset):
    middle = lax.optimization_barrier(jnp.mean(values, axis=-1, keepdims=True))
    centered = values - middle
    spread = lax.optimization_barrier(jnp.mean(centered * centered, axis=-1, keepdims=True))
    return centered * lax.rsqrt(spread + 1e-05) * gain_row + offset

def token_places(block_index):
    row_ids = jnp.arange(LEN, dtype=jnp.int32)
    return block_index[row_ids // HALF].astype(jnp.int32) * HALF + row_ids % HALF

def attention(queries, key_rows, value_rows, places):
    span_rows = math.gcd(LEN, 512)
    key_heads = key_rows.reshape(LEN, HEADS, HEAD_DIM)
    value_heads = value_rows.reshape(LEN, HEADS, HEAD_DIM)
    query_blocks = queries.reshape(LEN // span_rows, span_rows, HEADS, HEAD_DIM)
    place_blocks = places.reshape(LEN // span_rows, span_rows)

    def one_block(inputs):
        query_part, query_places = inputs
        scores = low_back(jnp.einsum('qhd,khd->hqk', query_part, key_heads, precision=lax.Precision.HIGHEST) * 0.125)
        visible = places[None, None, :] <= query_places[None, :, None]
        scores = jnp.where(visible, scores, -1e+30)
        row_max = lax.optimization_barrier(jnp.max(scores, axis=-1, keepdims=True))
        raised = jnp.exp(scores - row_max)
        weights = raised / lax.optimization_barrier(jnp.sum(raised, axis=-1, keepdims=True))
        return jnp.einsum('hqk,khd->qhd', low(weights), value_heads, precision=lax.Precision.HIGHEST)
    attended = lax.map(jax.checkpoint(one_block), (query_blocks, place_blocks))
    return attended.reshape(LEN, D)

def forward(tokens, norm_gains, norm_shifts, w_qkv, bias_model, w_out, w_up, bias_up, w_down, places):
    normed1 = low(layer_norm(tokens, norm_gains[0], norm_shifts[0]))
    no_key = jnp.zeros((D,), jnp.float32)
    qkv_bias = jnp.concatenate([bias_model[0], no_key, bias_model[1]])
    qkv_rows = low(low_back(matmul(normed1, w_qkv.T) + qkv_bias))
    attended = low(low_back(attention(qkv_rows[:, :D], qkv_rows[:, D:2 * D], qkv_rows[:, 2 * D:], places)))
    resid = tokens + low_back(matmul(attended, w_out.T) + bias_model[2])
    normed2 = low(layer_norm(resid, norm_gains[1], norm_shifts[1]))
    up_pre = low_back(matmul(normed2, w_up.T) + bias_up)
    act = low(jax.nn.gelu(up_pre, approximate=True))
    return resid + low_back(matmul(act, w_down.T) + bias_model[3])

def reference(tokens_in, block_index, norm_gains, norm_shifts, w_qkv, bias_model, w_out, w_up, bias_up, w_down, cotangent):
    places = token_places(block_index)
    params = (norm_gains.astype(jnp.float32), norm_shifts.astype(jnp.float32), w_qkv.astype(jnp.float32), bias_model.astype(jnp.float32), w_out.astype(jnp.float32), w_up.astype(jnp.float32), bias_up.astype(jnp.float32), w_down.astype(jnp.float32))

    def block_layer(tokens, *weights):
        return forward(tokens, *weights, places)

    def one_sequence(totals, inputs):
        tokens, seq_cotangent = inputs
        result, pullback = jax.vjp(block_layer, tokens.astype(jnp.float32), *params)
        gradients = pullback(seq_cotangent.astype(jnp.float32))
        totals = tuple((first + second for first, second in zip(totals, gradients[1:])))
        return (totals, (result.astype(jnp.bfloat16), gradients[0]))
    starting = tuple((jnp.zeros_like(item) for item in params))
    totals, (outputs, grad_tokens) = lax.scan(one_sequence, starting, (tokens_in, cotangent))
    return (outputs, grad_tokens, totals[0], totals[1], totals[2], totals[3], totals[4], totals[5], totals[6], totals[7])
```

```python
import functools
import math

import jax
import jax.numpy as jnp
import numpy as np
from jax import lax
from jax.experimental import pallas as pl
from jax.experimental.pallas import tpu as pltpu
from jax.sharding import PartitionSpec as P

HEADS = 25
HEAD_DIM = 64
LOG2E = 1.4426950408889634
NEGATIVE = -1e30
VMEM_LIMIT = 56 * 1024 * 1024


def layer_norm(values, gain_row, offset):
    middle = jnp.mean(values, axis=-1, keepdims=True)
    centered = values - middle
    spread = jnp.mean(centered * centered, axis=-1, keepdims=True)
    return centered * lax.rsqrt(spread + 1e-05) * gain_row + offset


def contract_last(left, right):
    return lax.dot_general(
        left, right, (((1,), (1,)), ((), ())), preferred_element_type=jnp.float32
    )


def contract_first(left, right):
    return lax.dot_general(
        left, right, (((0,), (0,)), ((), ())), preferred_element_type=jnp.float32
    )


class HeadPlan:
    def __init__(self, seq_size, ctx_size, shard_rows, width):
        first = [HEADS * c // ctx_size for c in range(ctx_size + 1)]
        self.slots = max(first[c + 1] - first[c] for c in range(ctx_size))
        self.count = [first[c + 1] - first[c] for c in range(ctx_size)]
        self.window = [min(first[c], HEADS - self.slots) for c in range(ctx_size)]
        self.skip = [first[c] - self.window[c] for c in range(ctx_size)]
        self.rows = self.slots * HEAD_DIM
        rows = self.rows
        self.piece_start = np.zeros((seq_size, ctx_size), np.int32)
        self.range_from = np.zeros((ctx_size, 3), np.int32)
        self.piece_from = np.zeros((ctx_size, seq_size), np.int32)
        self.source_row = np.zeros((seq_size, shard_rows), np.int32)
        for c in range(ctx_size):
            for t in range(3):
                begin = t * width + self.window[c] * HEAD_DIM
                for z in range(seq_size):
                    low, high = z * shard_rows, (z + 1) * shard_rows
                    if begin + rows <= low or begin >= high:
                        continue
                    start = min(max(begin, low), high - rows)
                    self.piece_start[z, c] = start - low
                    self.piece_from[c, z] = rows + t * rows + start - begin
                    if low <= begin < high:
                        self.range_from[c, t] = z * rows + begin - start
                used = t * width + first[c] * HEAD_DIM
                for row in range(used, used + self.count[c] * HEAD_DIM):
                    z = row // shard_rows
                    inside = row - z * shard_rows
                    self.source_row[z, inside] = c * rows + inside - self.piece_start[z, c]


def attention_forward_kernel(order_ref, q_ref, k_ref, v_ref, out_ref, qs, ks, vs, *, half, tile):
    length = q_ref.shape[0]
    for p in range(length // half):
        rows = pl.ds(pl.multiple_of(order_ref[p] * half, half), half)
        here = slice(p * half, (p + 1) * half)
        qs[here, :] = q_ref[rows, :]
        ks[here, :] = k_ref[rows, :]
        vs[here, :] = v_ref[rows, :]
    visible = lax.broadcasted_iota(jnp.int32, (tile, tile), 1) <= lax.broadcasted_iota(
        jnp.int32, (tile, tile), 0
    )
    scale = 0.125 * LOG2E
    for i in range(length // tile):
        span = (i + 1) * tile
        outs = []
        for h in range(q_ref.shape[1] // HEAD_DIM):
            lanes = slice(h * HEAD_DIM, (h + 1) * HEAD_DIM)
            q = qs[i * tile : span, lanes]
            scores = contract_last(q, ks[:span, lanes])
            last = jnp.where(visible, scores[:, i * tile :], NEGATIVE)
            scores = jnp.concatenate([scores[:, : i * tile], last], axis=1) if i else last
            top = jnp.max(scores, axis=1, keepdims=True)
            raised = jnp.exp2(scores * scale - top * scale)
            total = jnp.sum(raised, axis=1, keepdims=True)
            weights = (raised * (1.0 / total)).astype(jnp.bfloat16)
            outs.append(
                jnp.dot(weights, vs[:span, lanes], preferred_element_type=jnp.float32)
            )
        merged = jnp.concatenate(outs, axis=1).astype(out_ref.dtype)
        for j in range(tile // half):
            rows = pl.ds(pl.multiple_of(order_ref[i * (tile // half) + j] * half, half), half)
            out_ref[rows, :] = merged[j * half : (j + 1) * half, :]


def attention_forward(order, qkv, half, window):
    length = qkv.shape[0]
    groups = window // 128
    tile = 2 * half
    spec = lambda t: pl.BlockSpec((length, 128), lambda g, order: (0, t * groups + g))
    pairs = groups * 2 * length * length // 2
    return pl.pallas_call(
        functools.partial(attention_forward_kernel, half=half, tile=tile),
        grid_spec=pltpu.PrefetchScalarGridSpec(
            num_scalar_prefetch=1,
            grid=(groups,),
            in_specs=[spec(0), spec(1), spec(2)],
            out_specs=pl.BlockSpec((length, 128), lambda g, order: (0, g)),
            scratch_shapes=[pltpu.VMEM((length, 128), jnp.bfloat16)] * 3,
        ),
        out_shape=jax.ShapeDtypeStruct((length, window), jnp.bfloat16),
        compiler_params=pltpu.CompilerParams(vmem_limit_bytes=VMEM_LIMIT),
        cost_estimate=pl.CostEstimate(
            flops=4 * pairs * HEAD_DIM * 4, bytes_accessed=length * window * 8, transcendentals=pairs
        ),
    )(order, qkv, qkv, qkv)


def attention_backward_kernel(
    order_ref, q_ref, k_ref, v_ref, d_ref, dq_ref, dk_ref, dv_ref, qs, ks, vs, ds, kt, dks, dvs, *, half, tile
):
    length = q_ref.shape[0]
    for p in range(length // half):
        rows = pl.ds(pl.multiple_of(order_ref[p] * half, half), half)
        here = slice(p * half, (p + 1) * half)
        qs[here, :] = q_ref[rows, :]
        ks[here, :] = k_ref[rows, :]
        vs[here, :] = v_ref[rows, :]
        ds[here, :] = d_ref[rows, :]
    kt[...] = ks[...].T
    dks[...] = jnp.zeros_like(dks)
    dvs[...] = jnp.zeros_like(dvs)
    visible = lax.broadcasted_iota(jnp.int32, (tile, tile), 0) <= lax.broadcasted_iota(
        jnp.int32, (tile, tile), 1
    )
    scale = 0.125 * LOG2E
    heads = q_ref.shape[1] // HEAD_DIM
    for i in range(length // tile):
        span = (i + 1) * tile
        outs, d_keys, d_values = [], [], []
        for h in range(heads):
            lanes = slice(h * HEAD_DIM, (h + 1) * HEAD_DIM)
            q = qs[i * tile : span, lanes]
            d_out = ds[i * tile : span, lanes]
            scores = contract_last(ks[:span, lanes], q)
            last = jnp.where(visible, scores[i * tile :, :], NEGATIVE)
            scores = jnp.concatenate([scores[: i * tile, :], last], axis=0) if i else last
            top = jnp.max(scores, axis=0, keepdims=True)
            raised = jnp.exp2(scores * scale - top * scale)
            weights = raised * (1.0 / jnp.sum(raised, axis=0, keepdims=True))
            d_weights = contract_last(vs[:span, lanes], d_out)
            row_dot = jnp.sum(weights * d_weights, axis=0, keepdims=True)
            d_scores = (weights * (d_weights - row_dot)).astype(jnp.bfloat16)
            d_values.append(
                jnp.dot(weights.astype(jnp.bfloat16), d_out, preferred_element_type=jnp.float32)
            )
            d_keys.append(jnp.dot(d_scores, q, preferred_element_type=jnp.float32))
            outs.append(
                jnp.dot(kt[lanes, :span], d_scores, preferred_element_type=jnp.float32)
            )
        dks[:span, :] += jnp.concatenate(d_keys, axis=1)
        dvs[:span, :] += jnp.concatenate(d_values, axis=1)
        merged = (jnp.concatenate(outs, axis=0) * 0.125).T.astype(dq_ref.dtype)
        for j in range(tile // half):
            rows = pl.ds(pl.multiple_of(order_ref[i * (tile // half) + j] * half, half), half)
            dq_ref[rows, :] = merged[j * half : (j + 1) * half, :]
    for p in range(length // half):
        rows = pl.ds(pl.multiple_of(order_ref[p] * half, half), half)
        here = slice(p * half, (p + 1) * half)
        dk_ref[rows, :] = (dks[here, :] * 0.125).astype(dk_ref.dtype)
        dv_ref[rows, :] = dvs[here, :].astype(dv_ref.dtype)


def attention_backward(order, qkv, d_attended, half, window):
    length = qkv.shape[0]
    groups = window // 128
    tile = 2 * half
    spec = lambda t: pl.BlockSpec((length, 128), lambda g, order: (0, t * groups + g))
    pairs = groups * 2 * length * length // 2
    return pl.pallas_call(
        functools.partial(attention_backward_kernel, half=half, tile=tile),
        grid_spec=pltpu.PrefetchScalarGridSpec(
            num_scalar_prefetch=1,
            grid=(groups,),
            in_specs=[spec(0), spec(1), spec(2), spec(0)],
            out_specs=[spec(0)] * 3,
            scratch_shapes=[pltpu.VMEM((length, 128), jnp.bfloat16)] * 4
            + [pltpu.VMEM((128, length), jnp.bfloat16)]
            + [pltpu.VMEM((length, 128), jnp.float32)] * 2,
        ),
        out_shape=[jax.ShapeDtypeStruct((length, window), jnp.bfloat16)] * 3,
        compiler_params=pltpu.CompilerParams(vmem_limit_bytes=VMEM_LIMIT),
        cost_estimate=pl.CostEstimate(
            flops=10 * pairs * HEAD_DIM * 4,
            bytes_accessed=length * window * 14,
            transcendentals=pairs,
        ),
    )(order, qkv, qkv, qkv, d_attended)


def per_device(
    tokens_in,
    block_index,
    norm_gains,
    norm_shifts,
    w_qkv,
    bias_model,
    w_out,
    w_up,
    bias_up,
    w_down,
    cotangent,
):
    seq_size, ctx_size = lax.axis_size("seq"), lax.axis_size("ctx")
    z, c = lax.axis_index("seq"), lax.axis_index("ctx")
    tok_rows, width = tokens_in.shape[1], tokens_in.shape[2]
    length = tok_rows * ctx_size
    half = length // block_index.shape[0]
    hidden = bias_up.shape[0]
    own_hidden = hidden // seq_size // ctx_size
    low = jnp.bfloat16

    plan = HeadPlan(seq_size, ctx_size, w_qkv.shape[0], width)
    window = plan.rows
    table = lambda values, *index: jnp.asarray(np.asarray(values, np.int32))[index]
    head_from = table(plan.window, c) * HEAD_DIM
    slot = jnp.arange(window, dtype=jnp.int32) // HEAD_DIM - table(plan.skip, c)
    used = (slot >= 0) & (slot < table(plan.count, c))
    order = jnp.sum(
        jnp.where(
            block_index[None, :] == jnp.arange(block_index.shape[0], dtype=jnp.int32)[:, None],
            jnp.arange(block_index.shape[0], dtype=jnp.int32)[None, :],
            0,
        ),
        axis=1,
    )

    gather_seq = lambda value: lax.all_gather(value, "seq", axis=0, tiled=True)
    qkv_pieces = gather_seq(
        lax.dynamic_slice_in_dim(w_qkv, table(plan.piece_start, z, c), window, 0)
    )
    own_qkv = jnp.concatenate(
        [
            lax.dynamic_slice_in_dim(qkv_pieces, table(plan.range_from, c, t), window, 0)
            for t in range(3)
        ]
    )
    own_out = gather_seq(
        jnp.where(used[None, :], lax.dynamic_slice_in_dim(w_out, head_from, window, 1), 0)
    )
    own_up = gather_seq(lax.dynamic_slice_in_dim(w_up, c * own_hidden, own_hidden, 0))
    split_hidden = lambda value: value.reshape(value.shape[0], seq_size, ctx_size, own_hidden)
    own_down = gather_seq(
        lax.dynamic_index_in_dim(split_hidden(w_down), c, 2, keepdims=False).reshape(
            w_down.shape[0], seq_size * own_hidden
        )
    )
    own_bias_up = lax.dynamic_index_in_dim(
        split_hidden(bias_up[None, :]), c, 2, keepdims=False
    ).reshape(-1)

    gather_ctx = lambda value: lax.all_gather(value, "ctx", axis=0, tiled=True)
    scatter_ctx = lambda value: lax.psum_scatter(
        value.astype(low), "ctx", scatter_dimension=0, tiled=True
    ).astype(jnp.float32)
    scatter_seq = lambda value: lax.psum_scatter(
        value.astype(low), "seq", scatter_dimension=0, tiled=True
    )

    tokens = tokens_in[0].astype(jnp.float32)
    normed1 = layer_norm(tokens, norm_gains[0], norm_shifts[0]).astype(low)
    all_normed1 = gather_ctx(normed1)
    own_bias = jnp.concatenate(
        [
            lax.dynamic_slice_in_dim(bias_model[0], head_from, window, 0),
            jnp.zeros((window,), jnp.float32),
            lax.dynamic_slice_in_dim(bias_model[1], head_from, window, 0),
        ]
    )
    qkv = (contract_last(all_normed1, own_qkv) + own_bias).astype(low)
    attended = attention_forward(order, qkv, half, window)
    resid = tokens + scatter_ctx(contract_last(attended, own_out)) + bias_model[2]
    normed2 = layer_norm(resid, norm_gains[1], norm_shifts[1]).astype(low)
    all_normed2 = gather_ctx(normed2)
    up_pre = contract_last(all_normed2, own_up) + own_bias_up
    act = jax.nn.gelu(up_pre, approximate=True).astype(low)
    down = scatter_ctx(contract_last(act, own_down))
    tokens_out = (resid + down + bias_model[3]).astype(low)[None]

    seq_cotangent = cotangent[0]
    all_cotangent = gather_ctx(seq_cotangent)
    cotangent_f = seq_cotangent.astype(jnp.float32)
    grad_down_bias = jnp.sum(cotangent_f, axis=0)
    grad_w_down = scatter_seq(contract_first(all_cotangent, act))
    d_act = jnp.dot(all_cotangent, own_down, preferred_element_type=jnp.float32)
    gelu_back = jax.vjp(lambda inner_up: jax.nn.gelu(inner_up, approximate=True), up_pre)[1]
    d_up = gelu_back(d_act)[0].astype(low)
    grad_up_bias = jnp.sum(d_up.astype(jnp.float32), axis=0)
    grad_w_up = scatter_seq(contract_first(d_up, all_normed2))
    d_normed2 = scatter_ctx(jnp.dot(d_up, own_up, preferred_element_type=jnp.float32))
    norm_back2 = jax.vjp(layer_norm, resid, norm_gains[1], norm_shifts[1])[1]
    d_resid_norm, grad_gain2, grad_shift2 = norm_back2(d_normed2)
    d_resid = cotangent_f + d_resid_norm
    d_branch = d_resid.astype(low)
    grad_out_bias = jnp.sum(d_branch.astype(jnp.float32), axis=0)
    all_branch = gather_ctx(d_branch)
    grad_w_out = scatter_seq(contract_first(all_branch, attended))
    d_attended = jnp.dot(all_branch, own_out, preferred_element_type=jnp.float32).astype(low)
    d_qkv = jnp.concatenate(attention_backward(order, qkv, d_attended, half, window), axis=1)
    sums = jnp.sum(d_qkv.astype(jnp.float32), axis=0)
    place = lambda part: lax.dynamic_update_slice(
        jnp.zeros((width,), jnp.float32), part, (head_from,)
    )
    grad_query_bias, grad_value_bias = place(sums[:window]), place(sums[2 * window :])
    part = contract_first(d_qkv, all_normed1).astype(low)
    part = jnp.pad(part, ((window, window), (0, 0)))
    grad_w_qkv = scatter_seq(
        jnp.concatenate(
            [
                lax.dynamic_slice_in_dim(part, table(plan.piece_from, c, s), window, 0)
                for s in range(seq_size)
            ]
        )
    )
    d_normed1 = scatter_ctx(jnp.dot(d_qkv, own_qkv, preferred_element_type=jnp.float32))
    norm_back1 = jax.vjp(layer_norm, tokens, norm_gains[0], norm_shifts[0])[1]
    d_tokens_norm, grad_gain1, grad_shift1 = norm_back1(d_normed1)
    grad_tokens = (d_resid + d_tokens_norm)[None]

    grad_w_up = gather_ctx(grad_w_up).astype(jnp.float32)
    gathered = lax.all_gather(grad_w_down, "ctx", axis=0)
    gathered = gathered.reshape(ctx_size, w_down.shape[0], seq_size, own_hidden)
    grad_w_down = (
        jnp.transpose(gathered, (1, 2, 0, 3)).reshape(w_down.shape).astype(jnp.float32)
    )
    gathered = lax.all_gather(grad_w_out, "ctx", axis=0)
    grad_w_out = jnp.concatenate(
        [
            gathered[i][
                :, plan.skip[i] * HEAD_DIM : (plan.skip[i] + plan.count[i]) * HEAD_DIM
            ]
            for i in range(ctx_size)
        ],
        axis=1,
    ).astype(jnp.float32)
    gathered = gather_ctx(grad_w_qkv)
    grain = math.gcd(w_qkv.shape[0], HEAD_DIM)
    groups = table(plan.source_row[:, ::grain] // grain, z)
    grad_w_qkv = (
        jnp.take(gathered.reshape(-1, grain, width), groups, axis=0)
        .reshape(w_qkv.shape)
        .astype(jnp.float32)
    )

    spread_up = jnp.zeros((seq_size, ctx_size, own_hidden), jnp.float32)
    grad_up_bias = lax.dynamic_update_slice(
        spread_up, grad_up_bias.reshape(seq_size, 1, own_hidden), (0, c, 0)
    ).reshape(-1)
    small = jnp.concatenate(
        [
            grad_gain1,
            grad_gain2,
            grad_shift1,
            grad_shift2,
            grad_query_bias,
            grad_value_bias,
            grad_out_bias,
            grad_down_bias,
            grad_up_bias,
        ]
    )
    small = lax.psum(small, ("seq", "ctx"))
    return (
        tokens_out,
        grad_tokens,
        small[: 2 * width].reshape(2, width),
        small[2 * width : 4 * width].reshape(2, width),
        grad_w_qkv,
        small[4 * width : 8 * width].reshape(4, width),
        grad_w_out,
        grad_w_up,
        small[8 * width :],
        grad_w_down,
    )


def solution(mesh):
    placed = (
        P("seq", "ctx", None),
        P(),
        P(),
        P(),
        P("seq", None),
        P(),
        P("seq", None),
        P("seq", None),
        P(),
        P("seq", None),
        P("seq", "ctx", None),
    )
    return jax.shard_map(
        per_device,
        mesh=mesh,
        in_specs=placed,
        out_specs=(
            P("seq", "ctx", None),
            P("seq", "ctx", None),
            P(),
            P(),
            P("seq", None),
            P(),
            P("seq", None),
            P("seq", None),
            P(),
            P("seq", None),
        ),
        check_vma=False,
    )
```

```python
import functools
import math

import jax
import jax.numpy as jnp
import numpy as np
from jax import lax
from jax.experimental import pallas as pl
from jax.experimental.pallas import tpu as pltpu
from jax.sharding import PartitionSpec as P

HEADS = 25
HEAD_DIM = 64
LOG2E = 1.4426950408889634
NEGATIVE = -1e30
VMEM_LIMIT = 56 * 1024 * 1024


def contract_last(left, right):
    return lax.dot_general(
        left, right, (((1,), (1,)), ((), ())), preferred_element_type=jnp.float32
    )


def contract_first(left, right):
    return lax.dot_general(
        left, right, (((0,), (0,)), ((), ())), preferred_element_type=jnp.float32
    )


class HeadPlan:
    def __init__(self, seq_size, ctx_size, shard_rows, width, plane, below):
        first = [HEADS * c // ctx_size for c in range(ctx_size + 1)]
        self.count = [first[c + 1] - first[c] for c in range(ctx_size)]
        self.groups = (max(self.count) + 1) // 2
        self.window = [min(first[c], HEADS - 2 * self.groups) for c in range(ctx_size)]
        self.skip = [first[c] - self.window[c] for c in range(ctx_size)]
        self.rows = rows = 2 * HEAD_DIM
        self.grain = grain = math.gcd(shard_rows, HEAD_DIM)
        self.piece_start = np.zeros((self.groups, seq_size, ctx_size), np.int32)
        self.range_from = np.zeros((self.groups, ctx_size, 3), np.int32)
        self.piece_from = np.zeros((self.groups, ctx_size, seq_size), np.int32)
        owner = np.zeros((seq_size, shard_rows // grain, 3), np.int32)
        for c in range(ctx_size):
            for t in range(3):
                for g in range(self.groups):
                    begin = t * width + (self.window[c] + 2 * g) * HEAD_DIM
                    for z in range(seq_size):
                        low, high = z * shard_rows, (z + 1) * shard_rows
                        if begin + rows <= low or begin >= high:
                            continue
                        start = min(max(begin, low), high - rows)
                        self.piece_start[g, z, c] = start - low
                        self.piece_from[g, c, z] = rows + t * rows + start - begin
                        if low <= begin < high:
                            self.range_from[g, c, t] = z * rows + begin - start
                for head in range(first[c], first[c + 1]):
                    g = (head - self.window[c]) // 2
                    for row in range(t * width + head * HEAD_DIM, t * width + (head + 1) * HEAD_DIM, grain):
                        z = row // shard_rows
                        inside = row - z * shard_rows
                        owner[z, inside // grain] = g, c, inside - self.piece_start[g, z, c]
        self.source = np.zeros((seq_size, ctx_size, shard_rows // grain), np.int32)
        for c in range(ctx_size):
            for z in range(seq_size):
                for block in range(shard_rows // grain):
                    g, other, inside = owner[z, block]
                    stride = rows + (0 if g else below)
                    place = g * ctx_size * (rows + below) + plane.place(other ^ c) * stride + inside
                    self.source[z, c, block] = place // grain


def after(value, *others):
    one = jnp.float32(1.0)
    for other in others:
        sign = jnp.where(other[(0,) * other.ndim] > 0, jnp.float32(1.0), jnp.float32(-1.0))
        one = one * (sign * sign)
    return value * one.astype(value.dtype)


class Plane:
    def __init__(self, size):
        self.size = size
        self.even = list(range(0, size, 2))
        self.slots = self.even + [s + 1 for s in self.even]

    def place(self, slot):
        return self.slots.index(slot)

    def move(self, value, bits):
        return lax.ppermute(value, "ctx", [(i, i ^ bits) for i in range(self.size)])

    def send(self, value):
        if len(self.even) != 4:
            return [value] + [self.move(value, s) for s in self.even[1:]]
        half = value.shape[0] // 2
        first, second = self.move(value, 2), self.move(value, 4)
        return [value, first, second, self.move(first[:half], 4), self.move(second[half:], 2)]

    def share(self, near, order=()):
        last = held(near[-1:], order) if order else near[-1:]
        return near + [self.move(piece, 1) for piece in near[:-1] + last]

    def gather(self, value):
        return self.share(self.send(value))

    def other_half(self, lefts, rights, transposed, order=()):
        return product_rows(lefts, rights, transposed, len(self.even), [], order)

    def halves(self, lefts, rights, transposed, sent, order=()):
        sent = [self.move(part, 1) for part in sent]
        return product_rows(lefts, rights, transposed, len(self.even), sent, order)

    def exchange(self, parts):
        return [parts[0]] + [self.move(parts[i], s) for i, s in enumerate(self.even) if s]

    def scatter(self, lefts, rights, transposed, sent):
        return self.exchange(self.halves(lefts, rights, transposed, sent))


def total_by_bits(value, axis, size):
    bit = 1
    while bit < size:
        value = value + lax.ppermute(value, axis, [(i, i ^ bit) for i in range(size)])
        bit *= 2
    return value


def turn(value, by, size):
    return lax.ppermute(value, "seq", [(i, (i + by) % size) for i in range(size)])


def spread_line(pieces, size):
    return [pieces[0]] + [turn(pieces[k], k, size) for k in range(1, size)]


def scatter_line(pieces, size, order=()):
    return add_up(spread_line(pieces, size), order)


VMEM, SMEM, ANY = pltpu.VMEM, pltpu.SMEM, pl.ANY


def cost(micros):
    return pl.CostEstimate(flops=int(micros * 1.15e9), bytes_accessed=1 << 16, transcendentals=0)


def call(kernel, operands, shapes, scratch=(), scalars=0, order=(), micros=3):
    spaces = [SMEM] * scalars + [VMEM] * (len(operands) - scalars) + [ANY] * len(order)
    skipped = len(order)

    def body(*refs):
        count = len(operands)
        kernel(*refs[:count], *refs[count + skipped :])

    return pl.pallas_call(
        body,
        in_specs=[pl.BlockSpec(memory_space=space) for space in spaces],
        out_specs=[pl.BlockSpec(memory_space=VMEM) for _ in shapes],
        out_shape=[jax.ShapeDtypeStruct(shape, dtype) for shape, dtype in shapes],
        scratch_shapes=list(scratch),
        compiler_params=pltpu.CompilerParams(vmem_limit_bytes=VMEM_LIMIT),
        cost_estimate=cost(micros),
    )(*operands, *order)


def held(values, order):
    count = len(values)
    kept = pl.pallas_call(
        lambda *refs: None,
        in_specs=[pl.BlockSpec(memory_space=ANY)] * (count + len(order)),
        out_specs=[pl.BlockSpec(memory_space=ANY)] * count,
        out_shape=[jax.ShapeDtypeStruct(value.shape, value.dtype) for value in values],
        input_output_aliases={i: i for i in range(count)},
    )(*values, *order)
    return list(kept)


def padded(width):
    return -(-width // 128) * 128


def movable(grain):
    return jnp.bfloat16 if grain % 16 == 0 else jnp.float32


def blocks_of(refs, rows=512):
    found, offset = [], 0
    for ref in refs:
        step = ref.shape[0] if ref.shape[0] <= rows else math.gcd(ref.shape[0], rows)
        for start in range(0, ref.shape[0], step):
            at = offset + start
            found.append((ref, slice(start, start + step), slice(at, at + step)))
        offset += ref.shape[0]
    return found


def copy_kernel(in_ref, out_ref):
    out_ref[:, : in_ref.shape[1]] = in_ref[...]


def copied(value, order):
    rows, width = value.shape
    return call(copy_kernel, [value], [((rows, padded(width)), value.dtype)], order=order)[0]


def pack(share, columns, parts, order=()):
    high, width = share.shape
    rows, wide = columns.shape[0] // parts, columns.shape[1]

    def kernel(share_ref, columns_ref, out_ref):
        out_ref[:high, :width] = share_ref[...]
        for i in range(parts):
            out_ref[high:, i * wide : (i + 1) * wide] = columns_ref[i * rows : (i + 1) * rows, :]

    shape = (high + rows, padded(width))
    return call(kernel, [share, columns], [(shape, share.dtype)], order=order)[0]


def unpack(gathered, high, wide, parts, seq_size):
    step = gathered.shape[0] // seq_size
    rows = step - high

    def kernel(in_ref, out_ref):
        for s in range(seq_size):
            for i in range(parts):
                at = (s * parts + i) * rows
                out_ref[at : at + rows, :] = in_ref[
                    s * step + high : (s + 1) * step, i * wide : (i + 1) * wide
                ]

    shape = (seq_size * parts * rows, wide)
    return call(kernel, [gathered], [(shape, gathered.dtype)])[0]


def total_of(refs, width=None):
    total = refs[0][:, :width].astype(jnp.float32)
    for ref in refs[1:]:
        total = total + ref[:, :width].astype(jnp.float32)
    return total


def add_kernel(*refs):
    refs[-1][...] = total_of(refs[:-1]).astype(refs[-1].dtype)


def add_up(parts, order=()):
    return call(add_kernel, parts, [(parts[0].shape, jnp.bfloat16)], order=order)[0]


def centre(values):
    centered = values - jnp.mean(values, axis=-1, keepdims=True)
    inverse = lax.rsqrt(jnp.mean(centered * centered, axis=-1, keepdims=True) + 1e-05)
    return centered * inverse, inverse


def norm_kernel(tokens_ref, gain_ref, shift_ref, out_ref):
    hat, _ = centre(tokens_ref[...].astype(jnp.float32))
    out_ref[:, : hat.shape[1]] = (hat * gain_ref[...] + shift_ref[...]).astype(out_ref.dtype)


def branch_kernel(tokens_ref, bias_ref, gain_ref, shift_ref, *refs):
    *parts, resid_ref, out_ref = refs
    resid = tokens_ref[...].astype(jnp.float32) + total_of(parts, bias_ref.shape[1]) + bias_ref[...]
    resid_ref[...] = resid
    hat, _ = centre(resid)
    out_ref[:, : hat.shape[1]] = (hat * gain_ref[...] + shift_ref[...]).astype(out_ref.dtype)


def norm_back(values, upstream, gain):
    hat, inverse = centre(values)
    d_hat = upstream * gain
    back = inverse * (
        d_hat
        - jnp.mean(d_hat, axis=-1, keepdims=True)
        - hat * jnp.mean(d_hat * hat, axis=-1, keepdims=True)
    )
    return back, jnp.sum(upstream * hat, axis=0), jnp.sum(upstream, axis=0)


def branch_back_kernel(resid_ref, cotangent_ref, gain_ref, *refs):
    *parts, d_resid_ref, d_branch_ref, sums_ref = refs
    cotangent = cotangent_ref[...].astype(jnp.float32)
    back, d_gain, d_shift = norm_back(
        resid_ref[...], total_of(parts, gain_ref.shape[1]), gain_ref[...]
    )
    d_resid = cotangent + back
    d_branch = d_resid.astype(jnp.bfloat16)
    d_resid_ref[...] = d_resid
    d_branch_ref[:, : d_branch.shape[1]] = d_branch
    sums_ref[0, :] = d_gain
    sums_ref[1, :] = d_shift
    sums_ref[2, :] = jnp.sum(d_branch.astype(jnp.float32), axis=0)
    sums_ref[3, :] = jnp.sum(cotangent, axis=0)


def output_kernel(resid_ref, bias_ref, *refs):
    total = resid_ref[...] + total_of(refs[:-1], bias_ref.shape[1]) + bias_ref[...]
    refs[-1][...] = total.astype(refs[-1].dtype)


def product_rows(lefts, rights, transposed, parts, received, order=()):
    length = lefts[0].shape[0]
    rows = length // 2 // parts
    steps = parts // 2
    wide = rights[0].shape[0 if transposed else 1]
    sent = padded(wide)
    multiply = contract_last if transposed else (
        lambda left, right: jnp.dot(left, right, preferred_element_type=jnp.float32)
    )
    skipped = 0 if received else steps

    def kernel(*refs):
        left_refs, right_refs = refs[: len(lefts)], refs[len(lefts) : 2 * len(lefts)]
        rest = refs[2 * len(lefts) + len(order) :]
        got_refs, out_refs = rest[: len(received)], rest[len(received) :]
        total = multiply(left_refs[0][...], right_refs[0][...])
        for left_ref, right_ref in zip(left_refs[1:], right_refs[1:]):
            total = total + multiply(left_ref[...], right_ref[...])
        for i in range(parts):

            @pl.when(pl.program_id(0) == i // 2)
            def _():
                part = total[(i % 2) * rows : (i % 2 + 1) * rows]
                if got_refs:
                    part = part + got_refs[i][:, :wide].astype(jnp.float32)
                out_refs[i][:, :wide] = part.astype(jnp.bfloat16)

    whole = pl.BlockSpec((rows, sent), lambda i: (0, 0))
    return pl.pallas_call(
        kernel,
        grid=(steps,),
        in_specs=[
            pl.BlockSpec((2 * rows, left.shape[1]), lambda i: (i + skipped, 0)) for left in lefts
        ]
        + [pl.BlockSpec(right.shape, lambda i: (0, 0)) for right in rights]
        + [pl.BlockSpec(memory_space=ANY) for _ in order]
        + [whole for _ in received],
        out_specs=[whole] * parts,
        out_shape=[jax.ShapeDtypeStruct((rows, sent), jnp.bfloat16)] * parts,
        compiler_params=pltpu.CompilerParams(vmem_limit_bytes=VMEM_LIMIT),
        cost_estimate=cost(1),
    )(*lefts, *rights, *order, *received)


def row_products(pieces, right, order=()):
    length, wide = sum(piece.shape[0] for piece in pieces), right.shape[1]

    def kernel(*refs):
        *piece_refs, right_ref, out_ref = refs
        for ref, at, here in blocks_of(piece_refs):
            out_ref[here, :] = jnp.dot(
                ref[at, : right_ref.shape[0]], right_ref[...], preferred_element_type=jnp.float32
            ).astype(out_ref.dtype)

    return call(
        kernel, [*pieces, right], [((length, wide), jnp.bfloat16)], order=order, micros=1
    )[0]


def hidden_layer(pieces, weight, bias, d_act):
    length, wide = d_act.shape

    def kernel(*refs):
        *piece_refs, weight_ref, bias_ref, d_ref, act_ref, d_up_ref, sums_ref = refs
        sums = jnp.zeros((1, wide), jnp.float32)
        root = math.sqrt(2.0 / math.pi)
        for ref, at, here in blocks_of(piece_refs):
            up = contract_last(ref[at, : weight_ref.shape[1]], weight_ref[...]) + bias_ref[...]
            square = up * up
            bent = jnp.tanh(root * up * (1.0 + 0.044715 * square))
            act_ref[here, :] = (0.5 * up * (1.0 + bent)).astype(act_ref.dtype)
            slope = 0.5 * (1.0 + bent) + 0.5 * up * (1.0 - bent * bent) * root * (
                1.0 + 3.0 * 0.044715 * square
            )
            d_up = (d_ref[here, :].astype(jnp.float32) * slope).astype(jnp.bfloat16)
            d_up_ref[here, :] = d_up
            sums = sums + jnp.sum(d_up.astype(jnp.float32), axis=0, keepdims=True)
        sums_ref[...] = sums

    return call(
        kernel,
        [*pieces, weight, bias, d_act],
        [((length, wide), jnp.bfloat16)] * 2 + [((1, wide), jnp.float32)],
        micros=20,
    )


def row_sums(lefts, rights, high, wide, order=(), starts=None, rows=0, margin=0, grain=16, extra=None, micros=1):
    length = sum(left.shape[0] for left in lefts)
    cut = starts is not None
    added = [] if extra is None else [extra]
    count = starts.shape[0] // (1 + len(added)) if cut else 1
    below = extra.shape[0] // count if added else 0

    def kernel(*refs):
        if cut:
            starts_ref, *refs = refs
        left_refs, right_refs = refs[: len(lefts)], refs[len(lefts) : len(lefts) + len(rights)]
        scratch = list(refs[len(lefts) + len(rights) :])
        extra_refs = [scratch.pop(0) for _ in added]
        out_refs = [scratch.pop(0) for _ in range(count)]
        out_ref = scratch.pop() if cut else out_refs[0]
        sides = []
        for parts, columns in ((left_refs, high), (right_refs, wide)):
            if len(parts) == 1:
                sides.append(parts[0])
                continue
            whole = scratch.pop(0)
            for ref, at, here in blocks_of(parts):
                whole[here, :] = ref[at, :columns]
            sides.append(whole)
        for start in range(0, high, 256):
            stop = min(start + 256, high)
            out_ref[margin + start : margin + stop, :wide] = contract_first(
                sides[0][:, start:stop], sides[1][:, :wide]
            ).astype(out_ref.dtype)
        if cut:
            if margin:
                nothing = jnp.zeros((margin, padded(wide)), out_ref.dtype)
                out_ref[:margin, :] = nothing
                out_ref[margin + high :, :] = nothing
            for i, piece_ref in enumerate(out_refs):
                at = pl.ds(pl.multiple_of(starts_ref[i], grain), rows)
                piece_ref[:rows, :] = out_ref[at, :].astype(piece_ref.dtype)
                for extra_ref in extra_refs:
                    at = pl.ds(pl.multiple_of(starts_ref[count + i] * below, 16), below)
                    piece_ref[rows:, :] = extra_ref[at, :]

    scratch = [
        pltpu.VMEM((length, columns), jnp.bfloat16)
        for columns, parts in ((high, lefts), (wide, rights))
        if len(parts) > 1
    ]
    if not cut:
        shape = (high, padded(wide))
        return call(
            kernel, [*lefts, *rights], [(shape, jnp.bfloat16)], scratch, order=order, micros=micros
        )[0]
    scratch.append(pltpu.VMEM((high + 2 * margin, padded(wide)), movable(grain)))
    shapes = [((rows + below, padded(wide)), jnp.bfloat16)] * count
    return call(
        kernel, [starts, *lefts, *rights, *added], shapes, scratch, scalars=1, order=order, micros=micros
    )


def folded_sums(lefts, right, high, blocks, width, order=()):
    length, wide = right.shape
    count, parts, rows = blocks
    step = -(-rows // 32) * 32

    def kernel(*refs):
        *left_refs, right_ref, out_ref, whole, result = refs
        for ref, at, here in blocks_of(left_refs):
            whole[here, :] = ref[at, :high]
        for start in range(0, high, 256):
            stop = min(start + 256, high)
            result[start:stop, :] = contract_first(whole[:, start:stop], right_ref[...]).astype(
                result.dtype
            )
        out_ref[...] = jnp.zeros_like(out_ref)
        for s in range(count):
            for i in range(parts):
                at = (s * parts + i) * rows
                out_ref[s * step : s * step + rows, i * wide : (i + 1) * wide] = result[
                    at : at + rows, :
                ]

    return call(
        kernel,
        [*lefts, right],
        [((count * step, padded(width)), jnp.bfloat16)],
        [pltpu.VMEM((length, high), jnp.bfloat16), pltpu.VMEM((high, wide), jnp.bfloat16)],
        order=order,
        micros=1,
    )[0]


def final_rows(at, sources, places, groups, grain, heads, blocks, wide):
    count = sources.shape[1]
    heights = [sum(piece.shape[0] for piece in pieces) for pieces in groups]
    pieces = [piece for group in groups for piece in group]
    _, parts, rows = blocks
    positions = places.shape[1]
    stride = heights[0] // positions

    def kernel(at_ref, source_ref, place_ref, *refs):
        *piece_refs, qkv_ref, out_ref, whole = refs
        for ref, rows_at, here in blocks_of(piece_refs):
            whole[here, :] = ref[rows_at, :].astype(whole.dtype)
        for g in range(count):
            from_row = pl.ds(pl.multiple_of(source_ref[at_ref[0] * count + g] * grain, grain), grain)
            qkv_ref[g * grain : (g + 1) * grain, :] = whole[from_row, :wide].astype(jnp.float32)
        for i in range(parts):
            columns = []
            for p, (skip, used) in enumerate(heads):
                slot = place_ref[at_ref[1] * positions + p]
                from_row = pl.ds(pl.multiple_of(slot * stride + 2 * HEAD_DIM, 16), rows)
                start = i * blocks[0] + skip * HEAD_DIM
                columns.append(whole[from_row, start : start + used * HEAD_DIM].astype(jnp.float32))
            out_ref[i * rows : (i + 1) * rows, :] = jnp.concatenate(columns, axis=1)

    return call(
        kernel,
        [
            at,
            jnp.asarray(sources.reshape(-1)),
            jnp.asarray(places.reshape(-1)),
            *pieces,
        ],
        [((count * grain, wide), jnp.float32), ((parts * rows, wide), jnp.float32)],
        [pltpu.VMEM((sum(heights), pieces[0].shape[1]), movable(grain))],
        scalars=3,
        micros=8,
    )


def last_kernel(tokens_ref, d_resid_ref, gain_ref, *refs, terms):
    *parts, out_ref, sums_ref, share_ref = refs
    share_ref[...] = total_of(parts[terms:]).astype(share_ref.dtype)
    back, d_gain, d_shift = norm_back(
        tokens_ref[...].astype(jnp.float32), total_of(parts[:terms], gain_ref.shape[1]), gain_ref[...]
    )
    out_ref[...] = d_resid_ref[...] + back
    sums_ref[0, :] = d_gain
    sums_ref[1, :] = d_shift


def widen(gathered, rows, wide, order=()):
    count, high, columns = gathered.shape
    step = 8 // math.gcd(rows, 8)

    def kernel(in_ref, *refs):
        out_ref = refs[-1]
        for i in range(step):
            out_ref[i * rows : (i + 1) * rows, :] = in_ref[i, :rows, :wide].astype(jnp.float32)

    return pl.pallas_call(
        kernel,
        grid=(count // step,),
        in_specs=[pl.BlockSpec((step, high, columns), lambda i: (i, 0, 0))]
        + [pl.BlockSpec(memory_space=ANY) for _ in order],
        out_specs=pl.BlockSpec((step * rows, wide), lambda i: (i, 0)),
        out_shape=jax.ShapeDtypeStruct((count * rows, wide), jnp.float32),
        compiler_params=pltpu.CompilerParams(vmem_limit_bytes=VMEM_LIMIT),
        cost_estimate=cost(8),
    )(gathered, *order)


def columns_kernel(at_ref, in_ref, out_ref, *, pieces):
    out_ref[...] = jnp.concatenate(
        [in_ref[i ^ at_ref[0], :, start:stop].astype(jnp.float32) for i, start, stop in pieces],
        axis=1,
    )


def join_columns(at, gathered, pieces):
    count, rows, columns = gathered.shape
    wide = sum(stop - start for _, start, stop in pieces)
    block = math.gcd(rows, 80)
    return pl.pallas_call(
        functools.partial(columns_kernel, pieces=pieces),
        grid_spec=pltpu.PrefetchScalarGridSpec(
            num_scalar_prefetch=1,
            grid=(rows // block,),
            in_specs=[pl.BlockSpec((count, block, columns), lambda i, at: (0, i, 0))],
            out_specs=pl.BlockSpec((block, wide), lambda i, at: (i, 0)),
        ),
        out_shape=jax.ShapeDtypeStruct((rows, wide), jnp.float32),
        compiler_params=pltpu.CompilerParams(vmem_limit_bytes=VMEM_LIMIT),
        cost_estimate=cost(1),
    )(at.reshape(1), gathered)


def attention_forward_kernel(order_ref, *refs, half, grain, seq_size):
    from_ref, *piece_refs, bias_ref, out_ref, qkv_ref, weight_ref, qs, ks, vs, whole = refs
    length, wide = out_ref.shape
    piece_refs, share_refs = piece_refs[:-1], piece_refs[-1:]
    part = share_refs[0].shape[0] // seq_size
    for i in range(seq_size):
        here = slice(i * wide, (i + 1) * wide)
        whole[here, :] = share_refs[0][i * part : i * part + wide, : whole.shape[1]].astype(whole.dtype)
    for t in range(3):
        at = pl.ds(pl.multiple_of(from_ref[t], grain), wide)
        weight_ref[t * wide : (t + 1) * wide, :] = whole[at, :].astype(weight_ref.dtype)
    tile = 2 * half
    for ref, at, here in blocks_of(piece_refs):
        qkv_ref[here, :] = (
            contract_last(ref[at, : weight_ref.shape[1]], weight_ref[...]) + bias_ref[...]
        ).astype(qkv_ref.dtype)
    for p in range(length // half):
        rows = pl.ds(pl.multiple_of(order_ref[p] * half, half), half)
        here = slice(p * half, (p + 1) * half)
        qs[here, :] = qkv_ref[rows, :wide]
        ks[here, :] = qkv_ref[rows, wide : 2 * wide]
        vs[here, :] = qkv_ref[rows, 2 * wide :]
    visible = lax.broadcasted_iota(jnp.int32, (tile, tile), 1) <= lax.broadcasted_iota(
        jnp.int32, (tile, tile), 0
    )
    scale = 0.125 * LOG2E
    for i in range(length // tile):
        span = (i + 1) * tile
        outs = []
        for h in range(wide // HEAD_DIM):
            lanes = slice(h * HEAD_DIM, (h + 1) * HEAD_DIM)
            q = qs[i * tile : span, lanes]
            scores = contract_last(q, ks[:span, lanes])
            last = jnp.where(visible, scores[:, i * tile :], NEGATIVE)
            scores = jnp.concatenate([scores[:, : i * tile], last], axis=1) if i else last
            top = jnp.max(scores, axis=1, keepdims=True)
            raised = jnp.exp2(scores * scale - top * scale)
            total = jnp.sum(raised, axis=1, keepdims=True)
            weights = (raised * (1.0 / total)).astype(jnp.bfloat16)
            outs.append(
                jnp.dot(weights, vs[:span, lanes], preferred_element_type=jnp.float32)
            )
        merged = jnp.concatenate(outs, axis=1).astype(out_ref.dtype)
        for j in range(tile // half):
            rows = pl.ds(pl.multiple_of(order_ref[i * (tile // half) + j] * half, half), half)
            out_ref[rows, :] = merged[j * half : (j + 1) * half, :]


def attention_forward(block_order, pieces, starts, shares, bias, width, half, grain, seq_size, order=()):
    length = sum(piece.shape[0] for piece in pieces)
    wide = bias.shape[1] // 3
    return call(
        functools.partial(attention_forward_kernel, half=half, grain=grain, seq_size=seq_size),
        [block_order, starts, *pieces, shares, bias],
        [
            ((length, wide), jnp.bfloat16),
            ((length, 3 * wide), jnp.bfloat16),
            ((3 * wide, width), jnp.bfloat16),
        ],
        [pltpu.VMEM((length, wide), jnp.bfloat16)] * 3
        + [pltpu.VMEM((seq_size * wide, width), movable(grain))],
        scalars=2,
        micros=20,
        order=order,
    )


def attention_backward_kernel(order_ref, *refs, half):
    *piece_refs, weight_ref, qkv_ref, out_ref, sums_ref, qs, ks, vs, ds, kt, dks, dvs, raw = refs
    length, wide = qs.shape
    tile = 2 * half
    for ref, at, here in blocks_of(piece_refs):
        raw[here, :] = jnp.dot(
            ref[at, : weight_ref.shape[0]], weight_ref[...], preferred_element_type=jnp.float32
        ).astype(raw.dtype)
    for p in range(length // half):
        rows = pl.ds(pl.multiple_of(order_ref[p] * half, half), half)
        here = slice(p * half, (p + 1) * half)
        qs[here, :] = qkv_ref[rows, :wide]
        ks[here, :] = qkv_ref[rows, wide : 2 * wide]
        vs[here, :] = qkv_ref[rows, 2 * wide :]
        ds[here, :] = raw[rows, :]
    kt[...] = ks[...].T
    dks[...] = jnp.zeros_like(dks)
    dvs[...] = jnp.zeros_like(dvs)
    visible = lax.broadcasted_iota(jnp.int32, (tile, tile), 0) <= lax.broadcasted_iota(
        jnp.int32, (tile, tile), 1
    )
    scale = 0.125 * LOG2E
    heads = wide // HEAD_DIM
    for i in range(length // tile):
        span = (i + 1) * tile
        outs, d_keys, d_values = [], [], []
        for h in range(heads):
            lanes = slice(h * HEAD_DIM, (h + 1) * HEAD_DIM)
            q = qs[i * tile : span, lanes]
            d_out = ds[i * tile : span, lanes]
            scores = contract_last(ks[:span, lanes], q)
            last = jnp.where(visible, scores[i * tile :, :], NEGATIVE)
            scores = jnp.concatenate([scores[: i * tile, :], last], axis=0) if i else last
            top = jnp.max(scores, axis=0, keepdims=True)
            raised = jnp.exp2(scores * scale - top * scale)
            weights = raised * (1.0 / jnp.sum(raised, axis=0, keepdims=True))
            d_weights = contract_last(vs[:span, lanes], d_out)
            row_dot = jnp.sum(weights * d_weights, axis=0, keepdims=True)
            d_scores = (weights * (d_weights - row_dot)).astype(jnp.bfloat16)
            d_values.append(
                jnp.dot(weights.astype(jnp.bfloat16), d_out, preferred_element_type=jnp.float32)
            )
            d_keys.append(jnp.dot(d_scores, q, preferred_element_type=jnp.float32))
            outs.append(
                jnp.dot(kt[lanes, :span], d_scores, preferred_element_type=jnp.float32)
            )
        dks[:span, :] += jnp.concatenate(d_keys, axis=1)
        dvs[:span, :] += jnp.concatenate(d_values, axis=1)
        merged = (jnp.concatenate(outs, axis=0) * 0.125).T.astype(out_ref.dtype)
        for j in range(tile // half):
            rows = pl.ds(pl.multiple_of(order_ref[i * (tile // half) + j] * half, half), half)
            out_ref[rows, :wide] = merged[j * half : (j + 1) * half, :]
    for p in range(length // half):
        rows = pl.ds(pl.multiple_of(order_ref[p] * half, half), half)
        here = slice(p * half, (p + 1) * half)
        out_ref[rows, wide : 2 * wide] = (dks[here, :] * 0.125).astype(out_ref.dtype)
        out_ref[rows, 2 * wide :] = dvs[here, :].astype(out_ref.dtype)


    sums_ref[...] = jnp.sum(out_ref[...].astype(jnp.float32), axis=0, keepdims=True)


def attention_backward(block_order, pieces, weight, qkv, half, order=()):
    length = qkv.shape[0]
    wide = weight.shape[1]
    return call(
        functools.partial(attention_backward_kernel, half=half),
        [block_order, *pieces, weight, qkv],
        [((length, 3 * wide), jnp.bfloat16), ((1, 3 * wide), jnp.float32)],
        [pltpu.VMEM((length, wide), jnp.bfloat16)] * 4
        + [pltpu.VMEM((wide, length), jnp.bfloat16)]
        + [pltpu.VMEM((length, wide), jnp.float32)] * 2
        + [pltpu.VMEM((length, wide), jnp.bfloat16)],
        scalars=1,
        micros=28,
        order=order,
    )


def per_device(
    tokens_in,
    block_index,
    norm_gains,
    norm_shifts,
    w_qkv,
    bias_model,
    w_out,
    w_up,
    bias_up,
    w_down,
    cotangent,
):
    seq_size, ctx_size = lax.axis_size("seq"), lax.axis_size("ctx")
    z, c = lax.axis_index("seq"), lax.axis_index("ctx")
    tok_rows, width = tokens_in.shape[1], tokens_in.shape[2]
    length = tok_rows * ctx_size
    half = length // block_index.shape[0]
    hidden = bias_up.shape[0]
    own_hidden = hidden // seq_size // ctx_size
    kept_hidden = -(-own_hidden // 16) * 16
    low = jnp.bfloat16

    plane = Plane(ctx_size)
    out_blocks = (seq_size, 5, w_out.shape[0] // 5)
    below = -(-out_blocks[2] // 32) * 32
    plan = HeadPlan(seq_size, ctx_size, w_qkv.shape[0], width, plane, below)
    groups, rows = plan.groups, plan.rows
    window = groups * rows
    table = lambda values, *index: jnp.asarray(np.asarray(values, np.int32))[index]
    head_from = table(plan.window, c) * HEAD_DIM
    slot = jnp.arange(window, dtype=jnp.int32) // HEAD_DIM - table(plan.skip, c)
    used = (slot >= 0) & (slot < table(plan.count, c))
    blocks = block_index.shape[0]
    numbers = jnp.arange(blocks, dtype=jnp.int32)
    place_of = np.zeros((ctx_size, blocks), np.int32)
    for at in range(ctx_size):
        for b in range(blocks):
            place_of[at, b] = plane.place((b // 2) ^ at) * 2 + b % 2
    order = jnp.sum(
        jnp.where(block_index[None, :] == numbers[:, None], table(place_of, c)[None, :], 0), axis=1
    )
    row = lambda value: value.reshape(1, -1)
    shape, wide_shape = (tok_rows, width), (tok_rows, padded(width))

    tokens, own_cotangent = tokens_in[0], cotangent[0]
    gather_seq = lambda value: lax.all_gather(value, "seq", axis=0, tiled=True)
    shares = [
        lax.dynamic_slice_in_dim(w_qkv, table(plan.piece_start, g, z, c), rows, 0)
        for g in range(groups)
    ]
    normed1 = call(
        norm_kernel, [tokens, row(norm_gains[0]), row(norm_shifts[0])], [(wide_shape, low)]
    )[0]
    all_normed1 = plane.gather(normed1)
    out_share = jnp.where(
        used[None, :], lax.dynamic_slice_in_dim(w_out, head_from, window, 1), 0
    )
    shares[-1] = pack(shares[-1], out_share, 5, [normed1])
    qkv_pieces = [gather_seq(share) for share in shares]
    own_out = unpack(qkv_pieces[-1], rows, window, 5, seq_size)
    up_share = lax.dynamic_slice_in_dim(w_up, c * own_hidden, own_hidden, 0)
    fill = lambda value, axis: jnp.pad(
        value, [(0, kept_hidden - own_hidden if i == axis else 0) for i in range(value.ndim)]
    )
    up_share = fill(up_share, 0)
    down_share = jnp.concatenate(
        [
            fill(lax.dynamic_slice_in_dim(w_down, (s * ctx_size + c) * own_hidden, own_hidden, 1), 1)
            for s in range(seq_size)
        ],
        axis=1,
    )
    own_down = gather_seq(after(down_share, qkv_pieces[0]))
    own_up = gather_seq(after(up_share, qkv_pieces[0]))
    own_bias_up = jnp.concatenate(
        [
            fill(lax.dynamic_slice_in_dim(bias_up, (s * ctx_size + c) * own_hidden, own_hidden, 0), 0)
            for s in range(seq_size)
        ]
    )

    attended, qkv, own_qkv = [], [], []
    for g in range(groups):
        from_head = head_from + g * rows
        own_bias = jnp.concatenate(
            [
                lax.dynamic_slice_in_dim(bias_model[0], from_head, rows, 0),
                jnp.zeros((rows,), jnp.float32),
                lax.dynamic_slice_in_dim(bias_model[1], from_head, rows, 0),
            ]
        )
        if g == groups - 1:
            near = plane.send(copied(own_cotangent, all_normed1[-1:]))
            all_cotangent = plane.share(held(near, attended) if attended else near)
        out, kept, weight = attention_forward(
            order,
            all_normed1,
            table(plan.range_from, g, c),
            qkv_pieces[g],
            row(own_bias),
            width,
            half,
            plan.grain,
            seq_size,
            attended and all_cotangent[-1:],
        )
        own_qkv.append(weight)
        attended.append(out)
        qkv.append(kept)
    own_outs = [own_out[:, g * rows : (g + 1) * rows] for g in range(groups)]
    sent = plane.other_half(attended, own_outs, True)
    parts = plane.scatter(attended, own_outs, True, sent)
    d_act = row_products(all_cotangent, own_down)
    resid, normed2 = call(
        branch_kernel,
        [tokens, row(bias_model[2]), row(norm_gains[1]), row(norm_shifts[1]), *parts],
        [(shape, jnp.float32), (wide_shape, low)],
        order=[d_act],
    )
    all_normed2 = plane.gather(normed2)
    act, d_up, grad_up_bias = hidden_layer(all_normed2, own_up, row(own_bias_up), d_act)

    sent = plane.other_half([d_up], [own_up], False)
    parts = plane.scatter([d_up], [own_up], False, sent)
    part_down = row_sums(all_cotangent, [act], width, act.shape[1], parts[:1])
    part_up = row_sums([d_up], all_normed2, act.shape[1], width, parts[:1])
    down_sent = plane.other_half([act], [own_down], True, parts[:1])
    scatter_seq = lambda value: lax.psum_scatter(value, "seq", scatter_dimension=0, tiled=True)
    d_resid, d_branch, sums2 = call(
        branch_back_kernel,
        [resid, own_cotangent, row(norm_gains[1]), *parts],
        [(shape, jnp.float32), (wide_shape, low), ((4, width), jnp.float32)],
        order=[part_down, part_up, down_sent[0]],
    )
    grad_w_down, grad_w_up = (scatter_seq(part) for part in held([part_down, part_up], [d_branch]))
    near_branch = plane.send(d_branch)
    down_parts = plane.halves([act], [own_down], True, down_sent)
    all_branch = plane.share(near_branch, down_parts[:1])
    down_parts = plane.exchange(held(down_parts, all_branch[-1:]))
    turned = plan.piece_from[:, :, (np.arange(seq_size)[:, None] + np.arange(seq_size)) % seq_size]
    gather_ctx = lambda value: lax.all_gather(value, "ctx", axis=0)
    round_from = (z + jnp.arange(seq_size, dtype=jnp.int32)) % seq_size
    d_qkv, d_sums, early = [], [], []
    later = attention_backward(order, all_branch, own_outs[0], qkv[0], half, down_parts[:1])
    for g in range(groups):
        out, sums = later
        starts, extra = table(turned, g, c, z), None
        if g == 0:
            extra = folded_sums(
                all_branch, jnp.concatenate(attended, axis=1), width, out_blocks, width, [out]
            )
            starts = jnp.concatenate([starts, round_from])
        pieces = row_sums(
            [out],
            all_normed1,
            out.shape[1],
            width,
            early,
            starts=starts,
            rows=rows,
            margin=rows,
            grain=plan.grain,
            extra=extra,
        )
        if g == 0:
            grad_w_down = gather_ctx(held([grad_w_down], pieces[:1])[0])
            tokens_out = call(
                output_kernel, [resid, row(bias_model[3]), *down_parts], [(shape, low)], order=pieces[:1]
            )[0][None]
        if g < groups - 1:
            later = attention_backward(
                order, all_branch, own_outs[g + 1], qkv[g + 1], half, [pieces[0], tokens_out]
            )
            early.append(scatter_line(pieces, seq_size, later[:1]))
        d_qkv.append(out)
        d_sums.append(sums)
    grad_w_up = gather_ctx(held([grad_w_up], pieces[:1])[0])
    sent = plane.other_half(d_qkv, own_qkv, False, pieces[:1])
    gathered = [plane.send(share) for share in early]
    parts = plane.exchange(plane.halves(d_qkv, own_qkv, False, sent))
    gathered = [plane.share(near) for near in gathered]
    grad_w_down = join_columns(
        jnp.int32(0),
        grad_w_down,
        [
            (i, s * kept_hidden, s * kept_hidden + own_hidden)
            for s in range(seq_size)
            for i in range(ctx_size)
        ],
    )
    terms = spread_line(pieces, seq_size)
    grad_tokens, sums1, share = call(
        functools.partial(last_kernel, terms=len(parts)),
        [tokens, d_resid, row(norm_gains[0]), *parts, *terms],
        [(shape, jnp.float32), ((2, width), jnp.float32), (terms[0].shape, low)],
        order=[grad_w_down] + [piece for group in gathered for piece in group[-1:]],
    )
    grad_tokens = grad_tokens[None]
    near = plane.send(share)
    gathered.append(plane.share(near))
    grad_w_up = widen(grad_w_up, own_hidden, width, near[1:3])
    grad_w_qkv, grad_w_out = final_rows(
        jnp.stack([z * ctx_size + c, c]),
        plan.source.reshape(seq_size * ctx_size, -1),
        np.array([[plane.place(i ^ at) for i in range(ctx_size)] for at in range(ctx_size)], np.int32),
        gathered,
        plan.grain,
        list(zip(plan.skip, plan.count)),
        (window, *out_blocks[1:]),
        width,
    )

    place = lambda t: lax.dynamic_update_slice(
        jnp.zeros((1, width), jnp.float32),
        jnp.concatenate([part[:, t * rows : (t + 1) * rows] for part in d_sums], axis=1),
        (0, head_from),
    )
    spread_up = jnp.zeros((seq_size, ctx_size, own_hidden), jnp.float32)
    grad_up_bias = lax.dynamic_update_slice(
        spread_up, grad_up_bias.reshape(seq_size, 1, kept_hidden)[:, :, :own_hidden], (0, c, 0)
    ).reshape(-1, width)
    small = jnp.concatenate(
        [sums1[:1], sums2[:1], sums1[1:], sums2[1:2], place(0), place(2), sums2[2:], grad_up_bias]
    )
    small = total_by_bits(total_by_bits(small, "ctx", ctx_size), "seq", seq_size)
    return (
        tokens_out,
        grad_tokens,
        small[:2],
        small[2:4],
        grad_w_qkv,
        small[4:8],
        grad_w_out,
        grad_w_up,
        small[8:].reshape(-1),
        grad_w_down,
    )


def solution(mesh):
    placed = (
        P("seq", "ctx", None),
        P(),
        P(),
        P(),
        P("seq", None),
        P(),
        P("seq", None),
        P("seq", None),
        P(),
        P("seq", None),
        P("seq", "ctx", None),
    )
    return jax.shard_map(
        per_device,
        mesh=mesh,
        in_specs=placed,
        out_specs=(
            P("seq", "ctx", None),
            P("seq", "ctx", None),
            P(),
            P(),
            P("seq", None),
            P(),
            P("seq", None),
            P("seq", None),
            P(),
            P("seq", None),
        ),
        check_vma=False,
    )
```

```python
import functools
import math

import jax
import jax.numpy as jnp
import numpy as np
from jax import lax
from jax.experimental import pallas as pl
from jax.experimental.pallas import tpu as pltpu
from jax.sharding import PartitionSpec as P

HEADS = 25
HEAD_DIM = 64
LOG2E = 1.4426950408889634
NEGATIVE = -1e30
VMEM_LIMIT = 56 * 1024 * 1024


def contract_last(left, right):
    return lax.dot_general(
        left, right, (((1,), (1,)), ((), ())), preferred_element_type=jnp.float32
    )


def contract_first(left, right):
    return lax.dot_general(
        left, right, (((0,), (0,)), ((), ())), preferred_element_type=jnp.float32
    )


class HeadPlan:
    def __init__(self, seq_size, ctx_size, shard_rows, width, plane, below):
        first = [HEADS * c // ctx_size for c in range(ctx_size + 1)]
        self.count = [first[c + 1] - first[c] for c in range(ctx_size)]
        self.groups = (max(self.count) + 1) // 2
        self.window = [min(first[c], HEADS - 2 * self.groups) for c in range(ctx_size)]
        self.skip = [first[c] - self.window[c] for c in range(ctx_size)]
        self.rows = rows = 2 * HEAD_DIM
        self.grain = grain = math.gcd(shard_rows, HEAD_DIM)
        self.piece_start = np.zeros((self.groups, seq_size, ctx_size), np.int32)
        self.range_from = np.zeros((self.groups, ctx_size, 3), np.int32)
        self.piece_from = np.zeros((self.groups, ctx_size, seq_size), np.int32)
        owner = np.zeros((seq_size, shard_rows // grain, 3), np.int32)
        for c in range(ctx_size):
            for t in range(3):
                for g in range(self.groups):
                    begin = t * width + (self.window[c] + 2 * g) * HEAD_DIM
                    for z in range(seq_size):
                        low, high = z * shard_rows, (z + 1) * shard_rows
                        if begin + rows <= low or begin >= high:
                            continue
                        start = min(max(begin, low), high - rows)
                        self.piece_start[g, z, c] = start - low
                        self.piece_from[g, c, z] = rows + t * rows + start - begin
                        if low <= begin < high:
                            self.range_from[g, c, t] = z * rows + begin - start
                for head in range(first[c], first[c + 1]):
                    g = (head - self.window[c]) // 2
                    for row in range(t * width + head * HEAD_DIM, t * width + (head + 1) * HEAD_DIM, grain):
                        z = row // shard_rows
                        inside = row - z * shard_rows
                        owner[z, inside // grain] = g, c, inside - self.piece_start[g, z, c]
        self.source = np.zeros((seq_size, ctx_size, shard_rows // grain), np.int32)
        for c in range(ctx_size):
            for z in range(seq_size):
                for block in range(shard_rows // grain):
                    g, other, inside = owner[z, block]
                    place = plane.place(other ^ c) * (self.groups * rows + below) + inside
                    place += g * rows + (below if g else 0)
                    self.source[z, c, block] = place // grain


def after(value, *others):
    one = jnp.float32(1.0)
    for other in others:
        sign = jnp.where(other[(0,) * other.ndim] > 0, jnp.float32(1.0), jnp.float32(-1.0))
        one = one * (sign * sign)
    return value * one.astype(value.dtype)


class Plane:
    def __init__(self, size):
        self.size = size
        self.even = list(range(0, size, 2))
        self.slots = self.even + [s + 1 for s in self.even]

    def place(self, slot):
        return self.slots.index(slot)

    def move(self, value, bits):
        return lax.ppermute(value, "ctx", [(i, i ^ bits) for i in range(self.size)])

    def send(self, value, order=()):
        if len(self.even) != 4:
            return [value] + [self.move(value, s) for s in self.even[1:]]
        half = value.shape[0] // 2
        first, second = self.move(value, 2), self.move(value, 4)
        if order:
            first, second = held([first, second], order)
        return [value, first, second, self.move(first[:half], 4), self.move(second[half:], 2)]

    def share(self, near, order=()):
        last = held(near[-1:], order) if order else near[-1:]
        return near + [self.move(piece, 1) for piece in near[:-1] + last]

    def gather(self, value):
        return self.share(self.send(value))

    def other_half(self, lefts, rights, transposed, order=()):
        return product_rows(lefts, rights, transposed, len(self.even), [], order)

    def halves(self, lefts, rights, transposed, sent, order=()):
        sent = [self.move(part, 1) for part in sent]
        return product_rows(lefts, rights, transposed, len(self.even), sent, order)

    def exchange(self, parts):
        return [parts[0]] + [self.move(parts[i], s) for i, s in enumerate(self.even) if s]

    def scatter(self, lefts, rights, transposed, sent):
        return self.exchange(self.halves(lefts, rights, transposed, sent))


def total_by_bits(value, axis, size):
    bit = 1
    while bit < size:
        value = value + lax.ppermute(value, axis, [(i, i ^ bit) for i in range(size)])
        bit *= 2
    return value


def turn(value, by, size):
    return lax.ppermute(value, "seq", [(i, (i + by) % size) for i in range(size)])


def spread_line(pieces, size):
    return [pieces[0]] + [turn(pieces[k], k, size) for k in range(1, size)]


def scatter_line(pieces, size, order=()):
    return add_up(spread_line(pieces, size), order)


VMEM, SMEM, ANY = pltpu.VMEM, pltpu.SMEM, pl.ANY


def cost(micros):
    return pl.CostEstimate(flops=int(micros * 1.15e9), bytes_accessed=1 << 16, transcendentals=0)


def call(kernel, operands, shapes, scratch=(), scalars=0, order=(), micros=3):
    spaces = [SMEM] * scalars + [VMEM] * (len(operands) - scalars) + [ANY] * len(order)
    skipped = len(order)

    def body(*refs):
        count = len(operands)
        kernel(*refs[:count], *refs[count + skipped :])

    return pl.pallas_call(
        body,
        in_specs=[pl.BlockSpec(memory_space=space) for space in spaces],
        out_specs=[pl.BlockSpec(memory_space=VMEM) for _ in shapes],
        out_shape=[jax.ShapeDtypeStruct(shape, dtype) for shape, dtype in shapes],
        scratch_shapes=list(scratch),
        compiler_params=pltpu.CompilerParams(vmem_limit_bytes=VMEM_LIMIT),
        cost_estimate=cost(micros),
    )(*operands, *order)


def held(values, order):
    count = len(values)
    kept = pl.pallas_call(
        lambda *refs: None,
        in_specs=[pl.BlockSpec(memory_space=ANY)] * (count + len(order)),
        out_specs=[pl.BlockSpec(memory_space=ANY)] * count,
        out_shape=[jax.ShapeDtypeStruct(value.shape, value.dtype) for value in values],
        input_output_aliases={i: i for i in range(count)},
    )(*values, *order)
    return list(kept)


def padded(width):
    return -(-width // 128) * 128


def movable(grain):
    return jnp.bfloat16 if grain % 16 == 0 else jnp.float32


def blocks_of(refs, rows=512):
    found, offset = [], 0
    for ref in refs:
        step = ref.shape[0] if ref.shape[0] <= rows else math.gcd(ref.shape[0], rows)
        for start in range(0, ref.shape[0], step):
            at = offset + start
            found.append((ref, slice(start, start + step), slice(at, at + step)))
        offset += ref.shape[0]
    return found


def copy_kernel(in_ref, out_ref):
    out_ref[:, : in_ref.shape[1]] = in_ref[...]


def copied(value, order):
    rows, width = value.shape
    return call(copy_kernel, [value], [((rows, padded(width)), value.dtype)], order=order)[0]


def pack(share, columns, parts):
    high, width = share.shape
    rows, wide = columns.shape[0] // parts, columns.shape[1]

    def kernel(share_ref, columns_ref, out_ref):
        out_ref[:high, :width] = share_ref[...]
        for i in range(parts):
            out_ref[high:, i * wide : (i + 1) * wide] = columns_ref[i * rows : (i + 1) * rows, :]

    shape = (high + rows, padded(width))
    return call(kernel, [share, columns], [(shape, share.dtype)])[0]


def unpack(gathered, high, wide, parts, seq_size):
    step = gathered.shape[0] // seq_size
    rows = step - high

    def kernel(in_ref, out_ref):
        for s in range(seq_size):
            for i in range(parts):
                at = (s * parts + i) * rows
                out_ref[at : at + rows, :] = in_ref[
                    s * step + high : (s + 1) * step, i * wide : (i + 1) * wide
                ]

    shape = (seq_size * parts * rows, wide)
    return call(kernel, [gathered], [(shape, gathered.dtype)])[0]


def total_of(refs, width=None):
    total = refs[0][:, :width].astype(jnp.float32)
    for ref in refs[1:]:
        total = total + ref[:, :width].astype(jnp.float32)
    return total


def add_kernel(*refs):
    refs[-1][...] = total_of(refs[:-1]).astype(refs[-1].dtype)


def add_up(parts, order=()):
    return call(add_kernel, parts, [(parts[0].shape, jnp.bfloat16)], order=order)[0]


def centre(values):
    centered = values - jnp.mean(values, axis=-1, keepdims=True)
    inverse = lax.rsqrt(jnp.mean(centered * centered, axis=-1, keepdims=True) + 1e-05)
    return centered * inverse, inverse


def norm_kernel(tokens_ref, gain_ref, shift_ref, out_ref):
    hat, _ = centre(tokens_ref[...].astype(jnp.float32))
    out_ref[:, : hat.shape[1]] = (hat * gain_ref[...] + shift_ref[...]).astype(out_ref.dtype)


def branch_kernel(tokens_ref, bias_ref, gain_ref, shift_ref, *refs):
    *parts, resid_ref, out_ref = refs
    resid = tokens_ref[...].astype(jnp.float32) + total_of(parts, bias_ref.shape[1]) + bias_ref[...]
    resid_ref[...] = resid
    hat, _ = centre(resid)
    out_ref[:, : hat.shape[1]] = (hat * gain_ref[...] + shift_ref[...]).astype(out_ref.dtype)


def norm_back(values, upstream, gain):
    hat, inverse = centre(values)
    d_hat = upstream * gain
    back = inverse * (
        d_hat
        - jnp.mean(d_hat, axis=-1, keepdims=True)
        - hat * jnp.mean(d_hat * hat, axis=-1, keepdims=True)
    )
    return back, jnp.sum(upstream * hat, axis=0), jnp.sum(upstream, axis=0)


def branch_back_kernel(resid_ref, cotangent_ref, gain_ref, *refs):
    *parts, d_resid_ref, d_branch_ref, sums_ref = refs
    cotangent = cotangent_ref[...].astype(jnp.float32)
    back, d_gain, d_shift = norm_back(
        resid_ref[...], total_of(parts, gain_ref.shape[1]), gain_ref[...]
    )
    d_resid = cotangent + back
    d_branch = d_resid.astype(jnp.bfloat16)
    d_resid_ref[...] = d_resid
    d_branch_ref[:, : d_branch.shape[1]] = d_branch
    sums_ref[0, :] = d_gain
    sums_ref[1, :] = d_shift
    sums_ref[2, :] = jnp.sum(d_branch.astype(jnp.float32), axis=0)
    sums_ref[3, :] = jnp.sum(cotangent, axis=0)


def output_kernel(resid_ref, bias_ref, *refs):
    total = resid_ref[...] + total_of(refs[:-1], bias_ref.shape[1]) + bias_ref[...]
    refs[-1][...] = total.astype(refs[-1].dtype)


def product_rows(lefts, rights, transposed, parts, received, order=()):
    length = lefts[0].shape[0]
    rows = length // 2 // parts
    steps = parts // 2
    wide = rights[0].shape[0 if transposed else 1]
    sent = padded(wide)
    multiply = contract_last if transposed else (
        lambda left, right: jnp.dot(left, right, preferred_element_type=jnp.float32)
    )
    skipped = 0 if received else steps

    def kernel(*refs):
        left_refs, right_refs = refs[: len(lefts)], refs[len(lefts) : 2 * len(lefts)]
        rest = refs[2 * len(lefts) + len(order) :]
        got_refs, out_refs = rest[: len(received)], rest[len(received) :]
        total = multiply(left_refs[0][...], right_refs[0][...])
        for left_ref, right_ref in zip(left_refs[1:], right_refs[1:]):
            total = total + multiply(left_ref[...], right_ref[...])
        for i in range(parts):

            @pl.when(pl.program_id(0) == i // 2)
            def _():
                part = total[(i % 2) * rows : (i % 2 + 1) * rows]
                if got_refs:
                    part = part + got_refs[i][:, :wide].astype(jnp.float32)
                out_refs[i][:, :wide] = part.astype(jnp.bfloat16)

    whole = pl.BlockSpec((rows, sent), lambda i: (0, 0))
    return pl.pallas_call(
        kernel,
        grid=(steps,),
        in_specs=[
            pl.BlockSpec((2 * rows, left.shape[1]), lambda i: (i + skipped, 0)) for left in lefts
        ]
        + [pl.BlockSpec(right.shape, lambda i: (0, 0)) for right in rights]
        + [pl.BlockSpec(memory_space=ANY) for _ in order]
        + [whole for _ in received],
        out_specs=[whole] * parts,
        out_shape=[jax.ShapeDtypeStruct((rows, sent), jnp.bfloat16)] * parts,
        compiler_params=pltpu.CompilerParams(vmem_limit_bytes=VMEM_LIMIT),
        cost_estimate=cost(1),
    )(*lefts, *rights, *order, *received)


def row_products(pieces, right, order=()):
    length, wide = sum(piece.shape[0] for piece in pieces), right.shape[1]

    def kernel(*refs):
        *piece_refs, right_ref, out_ref = refs
        for ref, at, here in blocks_of(piece_refs):
            out_ref[here, :] = jnp.dot(
                ref[at, : right_ref.shape[0]], right_ref[...], preferred_element_type=jnp.float32
            ).astype(out_ref.dtype)

    return call(
        kernel, [*pieces, right], [((length, wide), jnp.bfloat16)], order=order, micros=1
    )[0]


def hidden_layer(pieces, weight, bias, d_act):
    length, wide = d_act.shape

    def kernel(*refs):
        *piece_refs, weight_ref, bias_ref, d_ref, act_ref, d_up_ref, sums_ref = refs
        sums = jnp.zeros((1, wide), jnp.float32)
        root = math.sqrt(2.0 / math.pi)
        for ref, at, here in blocks_of(piece_refs):
            up = contract_last(ref[at, : weight_ref.shape[1]], weight_ref[...]) + bias_ref[...]
            square = up * up
            bent = jnp.tanh(root * up * (1.0 + 0.044715 * square))
            act_ref[here, :] = (0.5 * up * (1.0 + bent)).astype(act_ref.dtype)
            slope = 0.5 * (1.0 + bent) + 0.5 * up * (1.0 - bent * bent) * root * (
                1.0 + 3.0 * 0.044715 * square
            )
            d_up = (d_ref[here, :].astype(jnp.float32) * slope).astype(jnp.bfloat16)
            d_up_ref[here, :] = d_up
            sums = sums + jnp.sum(d_up.astype(jnp.float32), axis=0, keepdims=True)
        sums_ref[...] = sums

    return call(
        kernel,
        [*pieces, weight, bias, d_act],
        [((length, wide), jnp.bfloat16)] * 2 + [((1, wide), jnp.float32)],
        micros=20,
    )


def row_sums(lefts, rights, high, wide, order=(), starts=None, rows=0, margin=0, grain=16, micros=1):
    length = sum(left.shape[0] for left in lefts)
    cut = starts is not None
    count = starts.shape[0] if cut else 1

    def kernel(*refs):
        if cut:
            starts_ref, *refs = refs
        left_refs, right_refs = refs[: len(lefts)], refs[len(lefts) : len(lefts) + len(rights)]
        scratch = list(refs[len(lefts) + len(rights) :])
        out_refs = [scratch.pop(0) for _ in range(count)]
        out_ref = scratch.pop() if cut else out_refs[0]
        sides = []
        for parts, columns in ((left_refs, high), (right_refs, wide)):
            if len(parts) == 1:
                sides.append(parts[0])
                continue
            whole = scratch.pop(0)
            for ref, at, here in blocks_of(parts):
                whole[here, :] = ref[at, :columns]
            sides.append(whole)
        for start in range(0, high, 256):
            stop = min(start + 256, high)
            out_ref[margin + start : margin + stop, :wide] = contract_first(
                sides[0][:, start:stop], sides[1][:, :wide]
            ).astype(out_ref.dtype)
        if cut:
            if margin:
                nothing = jnp.zeros((margin, padded(wide)), out_ref.dtype)
                out_ref[:margin, :] = nothing
                out_ref[margin + high :, :] = nothing
            for i, piece_ref in enumerate(out_refs):
                at = pl.ds(pl.multiple_of(starts_ref[i], grain), rows)
                piece_ref[...] = out_ref[at, :].astype(piece_ref.dtype)

    scratch = [
        pltpu.VMEM((length, columns), jnp.bfloat16)
        for columns, parts in ((high, lefts), (wide, rights))
        if len(parts) > 1
    ]
    if not cut:
        shape = (high, padded(wide))
        return call(
            kernel, [*lefts, *rights], [(shape, jnp.bfloat16)], scratch, order=order, micros=micros
        )[0]
    scratch.append(pltpu.VMEM((high + 2 * margin, padded(wide)), movable(grain)))
    shapes = [((rows, padded(wide)), jnp.bfloat16)] * count
    return call(
        kernel, [starts, *lefts, *rights], shapes, scratch, scalars=1, order=order, micros=micros
    )


def final_rows(at, sources, places, pieces, grain, heads, blocks, wide, order=()):
    count = sources.shape[1]
    height = sum(piece.shape[0] for piece in pieces)
    _, parts, rows = blocks
    positions = places.shape[1]
    stride = height // positions

    def kernel(at_ref, source_ref, place_ref, *refs):
        *piece_refs, qkv_ref, out_ref, whole = refs
        for ref, rows_at, here in blocks_of(piece_refs):
            whole[here, :] = ref[rows_at, :].astype(whole.dtype)
        for g in range(count):
            from_row = pl.ds(pl.multiple_of(source_ref[at_ref[0] * count + g] * grain, grain), grain)
            qkv_ref[g * grain : (g + 1) * grain, :] = whole[from_row, :wide].astype(jnp.float32)
        for i in range(parts):
            columns = []
            for p, (skip, used) in enumerate(heads):
                slot = place_ref[at_ref[1] * positions + p]
                from_row = pl.ds(pl.multiple_of(slot * stride + 2 * HEAD_DIM, math.gcd(stride, 16)), rows)
                start = i * blocks[0] + skip * HEAD_DIM
                columns.append(whole[from_row, start : start + used * HEAD_DIM].astype(jnp.float32))
            out_ref[i * rows : (i + 1) * rows, :] = jnp.concatenate(columns, axis=1)

    return call(
        kernel,
        [
            at,
            jnp.asarray(sources.reshape(-1)),
            jnp.asarray(places.reshape(-1)),
            *pieces,
        ],
        [((count * grain, wide), jnp.float32), ((parts * rows, wide), jnp.float32)],
        [pltpu.VMEM((height, pieces[0].shape[1]), movable(grain))],
        scalars=3,
        order=order,
        micros=8,
    )


def join_shares(early, columns, parts, below, last, order=()):
    rows, width = last[0].shape
    high, wide = columns.shape[0] // parts, columns.shape[1]
    height = (len(early) + 1) * rows + below

    def kernel(*refs):
        *refs, out_ref = refs
        early_refs, columns_ref, last_refs = refs[: len(early)], refs[len(early)], refs[len(early) + 1 :]
        shares = [ref[...] for ref in early_refs] + [total_of(last_refs).astype(out_ref.dtype)]
        for g, share in enumerate(shares):
            at = g * rows + (below if g else 0)
            out_ref[at : at + rows, :] = share
        out_ref[rows : rows + below, :] = jnp.zeros((below, width), out_ref.dtype)
        for i in range(parts):
            out_ref[rows : rows + high, i * wide : (i + 1) * wide] = columns_ref[
                i * high : (i + 1) * high, :
            ]

    return call(kernel, [*early, columns, *last], [((height, width), jnp.bfloat16)], order=order)[0]


def last_kernel(tokens_ref, d_resid_ref, gain_ref, *refs):
    *parts, out_ref, sums_ref = refs
    back, d_gain, d_shift = norm_back(
        tokens_ref[...].astype(jnp.float32), total_of(parts, gain_ref.shape[1]), gain_ref[...]
    )
    out_ref[...] = d_resid_ref[...] + back
    sums_ref[0, :] = d_gain
    sums_ref[1, :] = d_shift


def widen(gathered, rows, wide, order=()):
    count, high, columns = gathered.shape
    step = 8 // math.gcd(rows, 8)

    def kernel(in_ref, *refs):
        out_ref = refs[-1]
        for i in range(step):
            out_ref[i * rows : (i + 1) * rows, :] = in_ref[i, :rows, :wide].astype(jnp.float32)

    return pl.pallas_call(
        kernel,
        grid=(count // step,),
        in_specs=[pl.BlockSpec((step, high, columns), lambda i: (i, 0, 0))]
        + [pl.BlockSpec(memory_space=ANY) for _ in order],
        out_specs=pl.BlockSpec((step * rows, wide), lambda i: (i, 0)),
        out_shape=jax.ShapeDtypeStruct((count * rows, wide), jnp.float32),
        compiler_params=pltpu.CompilerParams(vmem_limit_bytes=VMEM_LIMIT),
        cost_estimate=cost(8),
    )(gathered, *order)


def columns_kernel(at_ref, in_ref, out_ref, *, pieces):
    out_ref[...] = jnp.concatenate(
        [in_ref[i ^ at_ref[0], :, start:stop].astype(jnp.float32) for i, start, stop in pieces],
        axis=1,
    )


def join_columns(at, gathered, pieces):
    count, rows, columns = gathered.shape
    wide = sum(stop - start for _, start, stop in pieces)
    block = math.gcd(rows, 80)
    return pl.pallas_call(
        functools.partial(columns_kernel, pieces=pieces),
        grid_spec=pltpu.PrefetchScalarGridSpec(
            num_scalar_prefetch=1,
            grid=(rows // block,),
            in_specs=[pl.BlockSpec((count, block, columns), lambda i, at: (0, i, 0))],
            out_specs=pl.BlockSpec((block, wide), lambda i, at: (i, 0)),
        ),
        out_shape=jax.ShapeDtypeStruct((rows, wide), jnp.float32),
        compiler_params=pltpu.CompilerParams(vmem_limit_bytes=VMEM_LIMIT),
        cost_estimate=cost(1),
    )(at.reshape(1), gathered)


def attention_forward_kernel(order_ref, *refs, half, grain, seq_size):
    from_ref, *piece_refs, bias_ref, out_ref, qkv_ref, weight_ref, qs, ks, vs, whole = refs
    length, wide = out_ref.shape
    piece_refs, share_refs = piece_refs[:-1], piece_refs[-1:]
    part = share_refs[0].shape[0] // seq_size
    for i in range(seq_size):
        here = slice(i * wide, (i + 1) * wide)
        whole[here, :] = share_refs[0][i * part : i * part + wide, : whole.shape[1]].astype(whole.dtype)
    for t in range(3):
        at = pl.ds(pl.multiple_of(from_ref[t], grain), wide)
        weight_ref[t * wide : (t + 1) * wide, :] = whole[at, :].astype(weight_ref.dtype)
    tile = 2 * half
    for ref, at, here in blocks_of(piece_refs):
        qkv_ref[here, :] = (
            contract_last(ref[at, : weight_ref.shape[1]], weight_ref[...]) + bias_ref[...]
        ).astype(qkv_ref.dtype)
    for p in range(length // half):
        rows = pl.ds(pl.multiple_of(order_ref[p] * half, half), half)
        here = slice(p * half, (p + 1) * half)
        qs[here, :] = qkv_ref[rows, :wide]
        ks[here, :] = qkv_ref[rows, wide : 2 * wide]
        vs[here, :] = qkv_ref[rows, 2 * wide :]
    visible = lax.broadcasted_iota(jnp.int32, (tile, tile), 1) <= lax.broadcasted_iota(
        jnp.int32, (tile, tile), 0
    )
    scale = 0.125 * LOG2E
    for i in range(length // tile):
        span = (i + 1) * tile
        outs = []
        for h in range(wide // HEAD_DIM):
            lanes = slice(h * HEAD_DIM, (h + 1) * HEAD_DIM)
            q = qs[i * tile : span, lanes]
            scores = contract_last(q, ks[:span, lanes])
            last = jnp.where(visible, scores[:, i * tile :], NEGATIVE)
            scores = jnp.concatenate([scores[:, : i * tile], last], axis=1) if i else last
            top = jnp.max(scores, axis=1, keepdims=True)
            raised = jnp.exp2(scores * scale - top * scale)
            total = jnp.sum(raised, axis=1, keepdims=True)
            weights = (raised * (1.0 / total)).astype(jnp.bfloat16)
            outs.append(
                jnp.dot(weights, vs[:span, lanes], preferred_element_type=jnp.float32)
            )
        merged = jnp.concatenate(outs, axis=1).astype(out_ref.dtype)
        for j in range(tile // half):
            rows = pl.ds(pl.multiple_of(order_ref[i * (tile // half) + j] * half, half), half)
            out_ref[rows, :] = merged[j * half : (j + 1) * half, :]


def attention_forward(block_order, pieces, starts, shares, bias, width, half, grain, seq_size, order=()):
    length = sum(piece.shape[0] for piece in pieces)
    wide = bias.shape[1] // 3
    return call(
        functools.partial(attention_forward_kernel, half=half, grain=grain, seq_size=seq_size),
        [block_order, starts, *pieces, shares, bias],
        [
            ((length, wide), jnp.bfloat16),
            ((length, 3 * wide), jnp.bfloat16),
            ((3 * wide, width), jnp.bfloat16),
        ],
        [pltpu.VMEM((length, wide), jnp.bfloat16)] * 3
        + [pltpu.VMEM((seq_size * wide, width), movable(grain))],
        scalars=2,
        micros=20,
        order=order,
    )


def attention_backward_kernel(order_ref, *refs, half):
    *piece_refs, weight_ref, qkv_ref, out_ref, sums_ref, qs, ks, vs, ds, kt, dks, dvs, raw = refs
    length, wide = qs.shape
    tile = 2 * half
    for ref, at, here in blocks_of(piece_refs):
        raw[here, :] = jnp.dot(
            ref[at, : weight_ref.shape[0]], weight_ref[...], preferred_element_type=jnp.float32
        ).astype(raw.dtype)
    for p in range(length // half):
        rows = pl.ds(pl.multiple_of(order_ref[p] * half, half), half)
        here = slice(p * half, (p + 1) * half)
        qs[here, :] = qkv_ref[rows, :wide]
        ks[here, :] = qkv_ref[rows, wide : 2 * wide]
        vs[here, :] = qkv_ref[rows, 2 * wide :]
        ds[here, :] = raw[rows, :]
    kt[...] = ks[...].T
    dks[...] = jnp.zeros_like(dks)
    dvs[...] = jnp.zeros_like(dvs)
    visible = lax.broadcasted_iota(jnp.int32, (tile, tile), 0) <= lax.broadcasted_iota(
        jnp.int32, (tile, tile), 1
    )
    scale = 0.125 * LOG2E
    heads = wide // HEAD_DIM
    for i in range(length // tile):
        span = (i + 1) * tile
        outs, d_keys, d_values = [], [], []
        for h in range(heads):
            lanes = slice(h * HEAD_DIM, (h + 1) * HEAD_DIM)
            q = qs[i * tile : span, lanes]
            d_out = ds[i * tile : span, lanes]
            scores = contract_last(ks[:span, lanes], q)
            last = jnp.where(visible, scores[i * tile :, :], NEGATIVE)
            scores = jnp.concatenate([scores[: i * tile, :], last], axis=0) if i else last
            top = jnp.max(scores, axis=0, keepdims=True)
            raised = jnp.exp2(scores * scale - top * scale)
            weights = raised * (1.0 / jnp.sum(raised, axis=0, keepdims=True))
            d_weights = contract_last(vs[:span, lanes], d_out)
            row_dot = jnp.sum(weights * d_weights, axis=0, keepdims=True)
            d_scores = (weights * (d_weights - row_dot)).astype(jnp.bfloat16)
            d_values.append(
                jnp.dot(weights.astype(jnp.bfloat16), d_out, preferred_element_type=jnp.float32)
            )
            d_keys.append(jnp.dot(d_scores, q, preferred_element_type=jnp.float32))
            outs.append(
                jnp.dot(kt[lanes, :span], d_scores, preferred_element_type=jnp.float32)
            )
        dks[:span, :] += jnp.concatenate(d_keys, axis=1)
        dvs[:span, :] += jnp.concatenate(d_values, axis=1)
        merged = (jnp.concatenate(outs, axis=0) * 0.125).T.astype(out_ref.dtype)
        for j in range(tile // half):
            rows = pl.ds(pl.multiple_of(order_ref[i * (tile // half) + j] * half, half), half)
            out_ref[rows, :wide] = merged[j * half : (j + 1) * half, :]
    for p in range(length // half):
        rows = pl.ds(pl.multiple_of(order_ref[p] * half, half), half)
        here = slice(p * half, (p + 1) * half)
        out_ref[rows, wide : 2 * wide] = (dks[here, :] * 0.125).astype(out_ref.dtype)
        out_ref[rows, 2 * wide :] = dvs[here, :].astype(out_ref.dtype)


    sums_ref[...] = jnp.sum(out_ref[...].astype(jnp.float32), axis=0, keepdims=True)


def attention_backward(block_order, pieces, weight, qkv, half, order=()):
    length = qkv.shape[0]
    wide = weight.shape[1]
    return call(
        functools.partial(attention_backward_kernel, half=half),
        [block_order, *pieces, weight, qkv],
        [((length, 3 * wide), jnp.bfloat16), ((1, 3 * wide), jnp.float32)],
        [pltpu.VMEM((length, wide), jnp.bfloat16)] * 4
        + [pltpu.VMEM((wide, length), jnp.bfloat16)]
        + [pltpu.VMEM((length, wide), jnp.float32)] * 2
        + [pltpu.VMEM((length, wide), jnp.bfloat16)],
        scalars=1,
        micros=28,
        order=order,
    )


def per_device(
    tokens_in,
    block_index,
    norm_gains,
    norm_shifts,
    w_qkv,
    bias_model,
    w_out,
    w_up,
    bias_up,
    w_down,
    cotangent,
):
    seq_size, ctx_size = lax.axis_size("seq"), lax.axis_size("ctx")
    z, c = lax.axis_index("seq"), lax.axis_index("ctx")
    tok_rows, width = tokens_in.shape[1], tokens_in.shape[2]
    length = tok_rows * ctx_size
    half = length // block_index.shape[0]
    hidden = bias_up.shape[0]
    own_hidden = hidden // seq_size // ctx_size
    kept_hidden = -(-own_hidden // 16) * 16
    low = jnp.bfloat16

    plane = Plane(ctx_size)
    out_blocks = (seq_size, 5, w_out.shape[0] // 5)
    below = -(-out_blocks[2] // 32) * 32
    plan = HeadPlan(seq_size, ctx_size, w_qkv.shape[0], width, plane, below)
    groups, rows = plan.groups, plan.rows
    window = groups * rows
    table = lambda values, *index: jnp.asarray(np.asarray(values, np.int32))[index]
    head_from = table(plan.window, c) * HEAD_DIM
    slot = jnp.arange(window, dtype=jnp.int32) // HEAD_DIM - table(plan.skip, c)
    used = (slot >= 0) & (slot < table(plan.count, c))
    blocks = block_index.shape[0]
    numbers = jnp.arange(blocks, dtype=jnp.int32)
    place_of = np.zeros((ctx_size, blocks), np.int32)
    for at in range(ctx_size):
        for b in range(blocks):
            place_of[at, b] = plane.place((b // 2) ^ at) * 2 + b % 2
    order = jnp.sum(
        jnp.where(block_index[None, :] == numbers[:, None], table(place_of, c)[None, :], 0), axis=1
    )
    row = lambda value: value.reshape(1, -1)
    shape, wide_shape = (tok_rows, width), (tok_rows, padded(width))

    tokens, own_cotangent = tokens_in[0], cotangent[0]
    gather_seq = lambda value: lax.all_gather(value, "seq", axis=0, tiled=True)
    shares = [
        lax.dynamic_slice_in_dim(w_qkv, table(plan.piece_start, g, z, c), rows, 0)
        for g in range(groups)
    ]
    normed1 = call(
        norm_kernel, [tokens, row(norm_gains[0]), row(norm_shifts[0])], [(wide_shape, low)]
    )[0]
    all_normed1 = plane.gather(normed1)
    out_share = jnp.where(
        used[None, :], lax.dynamic_slice_in_dim(w_out, head_from, window, 1), 0
    )
    shares[0] = pack(shares[0], out_share, 5)
    qkv_pieces = [gather_seq(share) for share in shares]
    own_out = unpack(qkv_pieces[0], rows, window, 5, seq_size)
    up_share = lax.dynamic_slice_in_dim(w_up, c * own_hidden, own_hidden, 0)
    fill = lambda value, axis: jnp.pad(
        value, [(0, kept_hidden - own_hidden if i == axis else 0) for i in range(value.ndim)]
    )
    up_share = fill(up_share, 0)
    down_share = jnp.concatenate(
        [
            fill(lax.dynamic_slice_in_dim(w_down, (s * ctx_size + c) * own_hidden, own_hidden, 1), 1)
            for s in range(seq_size)
        ],
        axis=1,
    )
    own_down = gather_seq(after(down_share, qkv_pieces[0]))
    own_up = gather_seq(after(up_share, qkv_pieces[0]))
    own_bias_up = jnp.concatenate(
        [
            fill(lax.dynamic_slice_in_dim(bias_up, (s * ctx_size + c) * own_hidden, own_hidden, 0), 0)
            for s in range(seq_size)
        ]
    )

    attended, qkv, own_qkv = [], [], []
    for g in range(groups):
        from_head = head_from + g * rows
        own_bias = jnp.concatenate(
            [
                lax.dynamic_slice_in_dim(bias_model[0], from_head, rows, 0),
                jnp.zeros((rows,), jnp.float32),
                lax.dynamic_slice_in_dim(bias_model[1], from_head, rows, 0),
            ]
        )
        if g == groups - 1:
            near = plane.send(copied(own_cotangent, all_normed1[-1:]), attended)
            all_cotangent = plane.share(held(near, attended) if attended else near)
        out, kept, weight = attention_forward(
            order,
            all_normed1,
            table(plan.range_from, g, c),
            qkv_pieces[g],
            row(own_bias),
            width,
            half,
            plan.grain,
            seq_size,
            attended and all_cotangent[-1:],
        )
        own_qkv.append(weight)
        attended.append(out)
        qkv.append(kept)
    own_outs = [own_out[:, g * rows : (g + 1) * rows] for g in range(groups)]
    sent = plane.other_half(attended, own_outs, True)
    parts = plane.scatter(attended, own_outs, True, sent)
    d_act = row_products(all_cotangent, own_down)
    resid, normed2 = call(
        branch_kernel,
        [tokens, row(bias_model[2]), row(norm_gains[1]), row(norm_shifts[1]), *parts],
        [(shape, jnp.float32), (wide_shape, low)],
        order=[d_act],
    )
    all_normed2 = plane.gather(normed2)
    act, d_up, grad_up_bias = hidden_layer(all_normed2, own_up, row(own_bias_up), d_act)

    sent = plane.other_half([d_up], [own_up], False)
    parts = plane.scatter([d_up], [own_up], False, sent)
    part_down = row_sums(all_cotangent, [act], width, act.shape[1], parts[:1])
    part_up = row_sums([d_up], all_normed2, act.shape[1], width, parts[:1])
    down_sent = plane.other_half([act], [own_down], True, parts[:1])
    scatter_seq = lambda value: lax.psum_scatter(value, "seq", scatter_dimension=0, tiled=True)
    d_resid, d_branch, sums2 = call(
        branch_back_kernel,
        [resid, own_cotangent, row(norm_gains[1]), *parts],
        [(shape, jnp.float32), (wide_shape, low), ((4, width), jnp.float32)],
        order=[part_down, part_up, down_sent[0]],
    )
    grad_w_down, grad_w_up = (scatter_seq(part) for part in held([part_down, part_up], [d_branch]))
    near_branch = plane.send(d_branch)
    down_parts = plane.halves([act], [own_down], True, down_sent)
    all_branch = plane.share(near_branch, down_parts[:1])
    down_parts = plane.exchange(held(down_parts, all_branch))
    turned = plan.piece_from[:, :, (np.arange(seq_size)[:, None] + np.arange(seq_size)) % seq_size]
    gather_ctx = lambda value: lax.all_gather(value, "ctx", axis=0)
    d_qkv, d_sums, early = [], [], []
    later = attention_backward(order, all_branch, own_outs[0], qkv[0], half, down_parts[:1])
    for g in range(groups):
        out, sums = later
        behind = []
        if g == 0:
            part_out = row_sums(
                all_branch, [jnp.concatenate(attended, axis=1)], width, window, [out]
            )
            tokens_out = call(
                output_kernel, [resid, row(bias_model[3]), *down_parts], [(shape, low)], order=[part_out]
            )[0][None]
            behind = [tokens_out]
        d_qkv.append(out)
        d_sums.append(sums)
        if g == groups - 1:
            shares = [add_up(terms, [out]) for terms in early]
            sent = plane.other_half(d_qkv, own_qkv, False, shares)
            behind = [*behind, sent[0]]
        pieces = row_sums(
            [out],
            all_normed1,
            out.shape[1],
            width,
            behind,
            starts=table(turned, g, c, z),
            rows=rows,
            margin=rows,
            grain=plan.grain,
        )
        if g == 0:
            grad_w_down = gather_ctx(held([grad_w_down], pieces[:1])[0])
        if g < groups - 1:
            later = attention_backward(order, all_branch, own_outs[g + 1], qkv[g + 1], half, pieces[:1])
            early.append(spread_line(pieces, seq_size))
    grad_w_up = gather_ctx(held([grad_w_up], pieces[:1])[0])
    halves = plane.halves(d_qkv, own_qkv, False, sent, [pieces[0], grad_w_down])
    parts = plane.exchange(halves)
    out_shard = scatter_seq(held([part_out], sent[:1])[0])
    share = join_shares(
        shares, out_shard, out_blocks[1], below, spread_line(pieces, seq_size), halves[:1]
    )
    gathered = plane.gather(share)
    grad_w_down = join_columns(
        jnp.int32(0),
        grad_w_down,
        [
            (i, s * kept_hidden, s * kept_hidden + own_hidden)
            for s in range(seq_size)
            for i in range(ctx_size)
        ],
    )
    grad_tokens, sums1 = call(
        last_kernel,
        [tokens, d_resid, row(norm_gains[0]), *parts],
        [(shape, jnp.float32), ((2, width), jnp.float32)],
        order=[grad_w_down],
    )
    grad_w_up = widen(grad_w_up, own_hidden, width)
    grad_tokens = grad_tokens[None]
    grad_w_qkv, grad_w_out = final_rows(
        jnp.stack([z * ctx_size + c, c]),
        plan.source.reshape(seq_size * ctx_size, -1),
        np.array(
            [
                [plane.place(i ^ at) for i in range(ctx_size)] for at in range(ctx_size)
            ],
            np.int32,
        ),
        gathered,
        plan.grain,
        list(zip(plan.skip, plan.count)),
        (window, *out_blocks[1:]),
        width,
        [grad_w_down, grad_w_up],
    )

    place = lambda t: lax.dynamic_update_slice(
        jnp.zeros((1, width), jnp.float32),
        jnp.concatenate([part[:, t * rows : (t + 1) * rows] for part in d_sums], axis=1),
        (0, head_from),
    )
    spread_up = jnp.zeros((seq_size, ctx_size, own_hidden), jnp.float32)
    grad_up_bias = lax.dynamic_update_slice(
        spread_up, grad_up_bias.reshape(seq_size, 1, kept_hidden)[:, :, :own_hidden], (0, c, 0)
    ).reshape(-1, width)
    small = jnp.concatenate(
        [sums1[:1], sums2[:1], sums1[1:], sums2[1:2], place(0), place(2), sums2[2:], grad_up_bias]
    )
    small = total_by_bits(total_by_bits(small, "ctx", ctx_size), "seq", seq_size)
    return (
        tokens_out,
        grad_tokens,
        small[:2],
        small[2:4],
        grad_w_qkv,
        small[4:8],
        grad_w_out,
        grad_w_up,
        small[8:].reshape(-1),
        grad_w_down,
    )


def solution(mesh):
    placed = (
        P("seq", "ctx", None),
        P(),
        P(),
        P(),
        P("seq", None),
        P(),
        P("seq", None),
        P("seq", None),
        P(),
        P("seq", None),
        P("seq", "ctx", None),
    )
    return jax.shard_map(
        per_device,
        mesh=mesh,
        in_specs=placed,
        out_specs=(
            P("seq", "ctx", None),
            P("seq", "ctx", None),
            P(),
            P(),
            P("seq", None),
            P(),
            P("seq", None),
            P("seq", None),
            P(),
            P("seq", None),
        ),
        check_vma=False,
    )
```
